128 devices in a mesh: section: 32 (over z, y, core), tensor: 4 (over x).
Axes of the slice: x: 4, y: 4, z: 4, core: 2. Of those that a mesh axis runs over, the one named last changes fastest.
Arguments:
- flight_state: bfloat16 [32, 512, 3584], P('section', 'tensor'), may hold values from -6 to 6
- flight_tokens: int32 [32, 3], P('section'), may hold values from 1 to 256, as said below
- flight_lists: int32 [32, 3], P('section'), may hold values from 0 to 1023, as said below
- incoming: bfloat16 [2, 512, 3584], P(None, 'tensor'), may hold values from -6 to 6
- incoming_tokens: int32 [2, 3], replicated, may hold values from 1 to 256, as said below
- norm_gain: float32 [32, 3584], P('section'), may hold values from 0.25 to 1.75
- query_weight: bfloat16 [32, 3584, 3584], P('section', None, 'tensor'), may hold values from -0.09375 to 0.09375
- query_bias: float32 [32, 3584], P('section', 'tensor'), may hold values from -10 to 10
- key_weight: bfloat16 [32, 3584, 512], P('section', None, 'tensor'), may hold values from -0.09375 to 0.09375
- key_bias: float32 [32, 512], P('section', 'tensor'), may hold values from -10 to 10
- value_weight: bfloat16 [32, 3584, 512], P('section', None, 'tensor'), may hold values from -0.09375 to 0.09375
- value_bias: float32 [32, 512], P('section', 'tensor'), may hold values from -3 to 3
- output_weight: bfloat16 [32, 3584, 3584], P('section', 'tensor'), may hold values from -0.09375 to 0.09375
- list_rows: int32 [1024], replicated, may hold values from 0 to 1023, each once
Outputs:
- next_state: bfloat16 [32, 512, 3584], P('section', 'tensor')
- list_sums: float32 [1024, 3584], P(('section', 'tensor'))
The draws below stay inside these ranges and needn't reach their ends.
Inputs may be any that keep to these rules, and one draw needn't show every extreme that they name: `flight_tokens`: in each micro-batch the blocks ceil(tokens / 128) of its 3 programs sum to 4; in every draw some program has the most and some program has 1 token. `incoming_tokens`: in each micro-batch the blocks ceil(tokens / 128) of its 3 programs sum to 4; in every draw some program has the most and some program has 1 token. `flight_lists`: every micro-batch after the first gives one of its programs the list of some program of the micro-batch before it.
All inputs are finite; a program needn't handle non-finite values.
Results may differ from the reference program's by a relative error of at most 0.034.
Values may be sent and summed in bfloat16 or wider, within the bound.
A program may use at most 128 MiB of HBM per device.

```python
import math
import jax
import jax.numpy as jnp
from jax import lax

D = 3584
HEADS = 28
KV_HEADS = 4
HEAD = 128
LAYERS = 28
ROWS = 512
BLOCK = 128
PROGS = 3
TICKS = 2
SECTIONS = 32
HEAD_GROUPS = 4
NLISTS = 1024


def program_tokens(key, count):
    keys = jax.random.split(jax.random.fold_in(key, 5), count)
    forced_index = jax.random.randint(jax.random.fold_in(key, 7), (), 0, count).astype(jnp.int32)
    forced = jnp.arange(count, dtype=jnp.int32) == forced_index

    def one_batch(single, is_forced):
        first_key, second_key, third_key = jax.random.split(single, 3)
        total_blocks = ROWS // BLOCK
        cuts = jnp.sort(jax.random.permutation(first_key, total_blocks - 1)[:PROGS - 1] + 1).astype(jnp.int32)
        edges = jnp.concatenate([jnp.zeros((1,), jnp.int32), cuts, jnp.full((1,), total_blocks, jnp.int32)])
        blocks = edges[1:] - edges[:-1]
        extra = jax.random.randint(second_key, (PROGS,), 1, BLOCK + 1).astype(jnp.int32)
        chosen = jax.random.randint(third_key, (), 0, PROGS).astype(jnp.int32)
        other = (chosen + 1) % PROGS
        index = jnp.arange(PROGS, dtype=jnp.int32)
        forced_blocks = jnp.where(index == chosen, total_blocks - (PROGS - 1), 1).astype(jnp.int32)
        forced_extra = jnp.where(index == chosen, BLOCK, jnp.where(index == other, 1, extra)).astype(jnp.int32)
        blocks = jnp.where(is_forced, forced_blocks, blocks)
        extra = jnp.where(is_forced, forced_extra, extra)
        return (blocks - 1) * BLOCK + extra
    return jax.vmap(one_batch)(keys, forced)


def draw_flight_tokens(key, part):
    return program_tokens(jax.random.fold_in(key, 11), SECTIONS)


def draw_incoming_tokens(key, part):
    return program_tokens(jax.random.fold_in(key, 23), TICKS)


def draw_flight_lists(key, part):
    drawn_lists = jax.random.randint(jax.random.fold_in(key, 83), (SECTIONS, PROGS), 0, NLISTS).astype(jnp.int32)
    column = jax.random.randint(jax.random.fold_in(key, 89), (SECTIONS,), 0, PROGS).astype(jnp.int32)
    offset = jax.random.randint(jax.random.fold_in(key, 97), (SECTIONS,), 0, PROGS - 1).astype(jnp.int32)
    high_row = jax.random.randint(jax.random.fold_in(key, 101), (), 0, SECTIONS).astype(jnp.int32)
    low_row = (high_row + 1) % SECTIONS
    index = jnp.arange(PROGS, dtype=jnp.int32)
    rows = jnp.arange(SECTIONS, dtype=jnp.int32)
    spare = (column + 1) % PROGS
    at_spare = index[None, :] == spare[:, None]
    drawn_lists = jnp.where((rows == high_row)[:, None] & at_spare, NLISTS - 1, drawn_lists)
    drawn_lists = jnp.where((rows == low_row)[:, None] & at_spare, 0, drawn_lists)
    source = (jnp.roll(column, 1) + 1 + offset) % PROGS
    previous_rows = jnp.roll(drawn_lists, 1, axis=0)
    shared = jnp.sum(jnp.where(index[None, :] == source[:, None], previous_rows, 0), axis=1)
    replace = (rows >= 1)[:, None] & (index[None, :] == column[:, None])
    return jnp.where(replace, shared[:, None], drawn_lists).astype(jnp.int32)


def draw_key_bias(key, part):
    shape = (SECTIONS, KV_HEADS * HEAD)
    return jnp.clip(0.5 * jax.random.normal(jax.random.fold_in(key, 73), shape, jnp.float32), -3.0, 3.0)


def draw_query_bias(key, part):
    shape = (SECTIONS, HEADS * HEAD)
    return jnp.clip(0.5 * jax.random.normal(jax.random.fold_in(key, 77), shape, jnp.float32), -3.0, 3.0)


def block_levels(rng, dims, pieces, low, high):
    level, own = 1.0, jax.random.fold_in(rng, 6)
    for axis_at, blocks in pieces:
        heights = jnp.exp(jax.random.uniform(jax.random.fold_in(own, axis_at), (blocks,), jnp.float32, low / len(pieces), high / len(pieces)))
        level = level * jnp.repeat(heights, dims[axis_at] // blocks).reshape([-1 if axis == axis_at else 1 for axis in range(len(dims))])
    return level


def centred(key, dims, scale, most, cuts=(), kind=jnp.bfloat16):
    result = scale * jax.random.normal(key, dims, jnp.float32)
    if cuts:
        result = result * block_levels(key, dims, cuts, -0.22, 0.18)
    return jnp.clip(result, -most, most).astype(kind)


def setup_inputs(seed: int = 0) -> dict:
    key_list = jax.random.split(jax.random.key(seed), 15)
    flight_state = centred(key_list[0], (SECTIONS, ROWS, D), 1.0, 6.0, ((0, 32), (1, 4)))
    flight_tokens = draw_flight_tokens(jax.random.fold_in(key_list[14], 71), 0)
    flight_lists = draw_flight_lists(jax.random.fold_in(key_list[14], 71), 0)
    incoming = centred(key_list[3], (TICKS, ROWS, D), 1.0, 6.0, ((1, 4),))
    incoming_tokens = draw_incoming_tokens(jax.random.fold_in(key_list[14], 71), 0)
    norm_gain = jnp.clip(1.0 + 0.15 * jax.random.normal(key_list[5], (SECTIONS, D), jnp.float32), 0.25, 1.75)
    query_weight = centred(key_list[6], (SECTIONS, D, HEADS * HEAD), D ** -0.5, 0.09375, ((0, 32), (2, 4)))
    query_bias = draw_query_bias(jax.random.fold_in(key_list[14], 71), 0)
    key_weight = centred(key_list[8], (SECTIONS, D, KV_HEADS * HEAD), D ** -0.5, 0.09375, ((0, 32), (2, 4)))
    key_bias = draw_key_bias(jax.random.fold_in(key_list[14], 71), 0)
    value_weight = centred(key_list[10], (SECTIONS, D, KV_HEADS * HEAD), D ** -0.5, 0.09375, ((0, 32), (2, 4)))
    value_bias = centred(key_list[11], (SECTIONS, KV_HEADS * HEAD), 0.5, 3.0, ((0, 32), (1, 4)), jnp.float32)
    output_weight = centred(key_list[12], (SECTIONS, HEADS * HEAD, D), (HEADS * HEAD) ** -0.5, 0.09375, ((0, 32), (1, 4)))
    list_rows = jax.random.permutation(key_list[13], NLISTS).astype(jnp.int32)
    return dict(flight_state=flight_state, flight_tokens=flight_tokens, flight_lists=flight_lists, incoming=incoming, incoming_tokens=incoming_tokens, norm_gain=norm_gain, query_weight=query_weight, query_bias=query_bias, key_weight=key_weight, key_bias=key_bias, value_weight=value_weight, value_bias=value_bias, output_weight=output_weight, list_rows=list_rows)


EPS = 1e-06
THETA = 1000000.0

def row_layout(tokens, first, count):
    blocks = (tokens + BLOCK - 1) // BLOCK
    ends = (jnp.cumsum(blocks) * BLOCK).astype(jnp.int32)
    starts = ends - blocks * BLOCK
    slots = first + jnp.arange(count, dtype=jnp.int32)
    program = lax.optimization_barrier(jnp.sum((slots[:, None] >= ends[None, :]).astype(jnp.int32), axis=1))
    chosen = program[:, None] == jnp.arange(tokens.shape[0], dtype=jnp.int32)[None, :]
    begin = lax.optimization_barrier(jnp.sum(jnp.where(chosen, starts[None, :], 0), axis=1))
    length = lax.optimization_barrier(jnp.sum(jnp.where(chosen, tokens[None, :], 0), axis=1))
    position = slots - begin
    return (program, position, position < length)

def rotate(values, position):
    half = values.shape[-1] // 2
    freq = THETA ** (-jnp.arange(half, dtype=jnp.float32) * 2.0 / values.shape[-1])
    angle = position.astype(jnp.float32)[:, None] * freq[None, :]
    cosine = jnp.cos(angle)[:, None, :]
    sine = jnp.sin(angle)[:, None, :]
    first_half = values[..., :half]
    second_half = values[..., half:]
    return jnp.concatenate([first_half * cosine - second_half * sine, second_half * cosine + first_half * sine], axis=-1)

def attend(queries, key_rows, value_rows, program, valid):
    total = queries.shape[0]
    width = min(512, total)
    scale = 1.0 / math.sqrt(queries.shape[-1])

    def one_block(index):
        block_q = lax.dynamic_slice_in_dim(queries, index * width, width, 0)
        block_p = lax.dynamic_slice_in_dim(program, index * width, width, 0)
        scores = jnp.einsum('qcgd,kcd->cgqk', block_q.astype(jnp.float32), key_rows.astype(jnp.float32)) * scale
        allowed = (block_p[:, None] == program[None, :]) & valid[None, :]
        scores = jnp.where(allowed[None, None], scores, -1e+30)
        top = lax.optimization_barrier(jnp.max(scores, axis=-1, keepdims=True))
        expo = jnp.exp(scores - top)
        probs = (expo / lax.optimization_barrier(jnp.sum(expo, axis=-1, keepdims=True))).astype(jnp.bfloat16)
        mixed = jnp.einsum('cgqk,kcd->qcgd', probs.astype(jnp.float32), value_rows.astype(jnp.float32))
        return mixed.astype(jnp.bfloat16)
    blocks = lax.map(one_block, jnp.arange(total // width, dtype=jnp.int32))
    return blocks.reshape(total, -1)

def layer(packed):
    state, tokens, gain, w_query, b_query, w_key, b_key, w_value, b_value, w_out = packed
    program, position, valid = row_layout(tokens, 0, ROWS)
    values = state.astype(jnp.float32)
    normed = (values * lax.rsqrt(lax.optimization_barrier(jnp.mean(values * values, axis=-1, keepdims=True)) + EPS) * gain).astype(jnp.bfloat16)
    query_f = jnp.dot(normed, w_query, preferred_element_type=jnp.float32) + b_query
    key_f = jnp.dot(normed, w_key, preferred_element_type=jnp.float32) + b_key
    value_f = jnp.dot(normed, w_value, preferred_element_type=jnp.float32) + b_value
    queries = rotate(query_f.reshape(ROWS, HEADS, HEAD), position).astype(jnp.bfloat16)
    queries = queries.reshape(ROWS, KV_HEADS, HEADS // KV_HEADS, HEAD)
    key_rows = rotate(key_f.reshape(ROWS, KV_HEADS, HEAD), position).astype(jnp.bfloat16)
    value_rows = value_f.astype(jnp.bfloat16).reshape(ROWS, KV_HEADS, HEAD)
    mixed = attend(queries, key_rows, value_rows, program, valid)
    group_cols = HEADS * HEAD // HEAD_GROUPS
    added = jnp.zeros((ROWS, D), jnp.float32)
    for group in range(HEAD_GROUPS):
        partial_term = jnp.dot(mixed[:, group * group_cols:(group + 1) * group_cols], w_out[group * group_cols:(group + 1) * group_cols], preferred_element_type=jnp.float32)
        added = added + lax.optimization_barrier(partial_term.astype(jnp.bfloat16)).astype(jnp.float32)
    return (values + added).astype(jnp.bfloat16)

def reference(flight_state, flight_tokens, flight_lists, incoming, incoming_tokens, norm_gain, query_weight, query_bias, key_weight, key_bias, value_weight, value_bias, output_weight, list_rows):
    state = flight_state
    tokens = flight_tokens
    lists = flight_lists
    live = jnp.arange(SECTIONS, dtype=jnp.int32) < min(SECTIONS, LAYERS)
    pooled_all = []
    lists_all = []
    for tick in range(TICKS):
        mapped = lax.map(layer, (state, tokens, norm_gain, query_weight, query_bias, key_weight, key_bias, value_weight, value_bias, output_weight))
        outputs = jnp.where(live[:, None, None], mapped, state)
        program, position, valid = row_layout(tokens[-1], 0, ROWS)
        member = ((program[None, :] == jnp.arange(PROGS, dtype=jnp.int32)[:, None]) & valid[None, :]).astype(jnp.bfloat16)
        summed = jnp.dot(member, outputs[-1], preferred_element_type=jnp.float32)
        pooled_all.append(summed / tokens[-1][:, None].astype(jnp.float32))
        lists_all.append(lists[-1])
        state = jnp.concatenate([incoming[tick][None], outputs[:-1]], axis=0)
        tokens = jnp.concatenate([incoming_tokens[tick][None], tokens[:-1]], axis=0)
        lists = jnp.concatenate([jnp.zeros((1, PROGS), jnp.int32), lists[:-1]], axis=0)
    means = jnp.stack(pooled_all)
    embedded = means * lax.rsqrt(lax.optimization_barrier(jnp.mean(means * means, axis=-1, keepdims=True)) + EPS)
    flat = embedded.reshape(-1, D)
    flat_lists = jnp.stack(lists_all).reshape(-1)
    target = lax.optimization_barrier(jnp.sum(jnp.where(flat_lists[:, None] == jnp.arange(NLISTS, dtype=jnp.int32)[None, :], list_rows[None, :], 0), axis=1))
    select = (jnp.arange(NLISTS, dtype=jnp.int32)[:, None] == target[None, :]).astype(jnp.float32)
    list_sums = jnp.dot(select, flat, precision=lax.Precision.HIGHEST)
    return (state, list_sums)
```

```python
import math

import jax
import jax.numpy as jnp
import numpy as np
from jax import lax
from jax.experimental import pallas as pl
from jax.experimental.pallas import tpu as pltpu
from jax.sharding import PartitionSpec as P

HEAD = 128
LAYERS = 28
BLOCK = 128
EPS = 1e-06
THETA = 1000000.0

NT = 4
NC = 4
CR = BLOCK // NC
HR = CR // 2
NEG = -1e30
MESH = pl.DeviceIdType.MESH


def rope_tables():
    half = HEAD // 2
    freq = THETA ** (-np.arange(half, dtype=np.float64) * 2.0 / HEAD)
    freq = freq.astype(np.float32).astype(np.float64)
    angle = np.arange(2 * BLOCK, dtype=np.float64)[:, None] * freq[None, :]
    cosine, sine = np.cos(angle), np.sin(angle)
    return (
        np.concatenate([cosine, cosine], 1).astype(np.float32),
        np.concatenate([-sine, sine], 1).astype(np.float32),
    )


def kernel(
    n_sections,
    n_layers,
    flight,
    tokens,
    lists,
    incoming,
    inc_tokens,
    gain,
    wq_hbm,
    qb,
    wk_hbm,
    kb,
    wv_hbm,
    vb,
    wo_hbm,
    list_rows,
    cos_tab,
    sin_tab,
    out,
    sums,
    w,
    wo,
    x,
    y,
    g,
    part,
    ra,
    rb,
    fl,
    fr,
    q_s,
    k_s,
    v_s,
    mixed,
    rc,
    rs,
    mask,
    tok,
    pool,
    pool_part,
    w_sem,
    x_sem,
    inc_sem,
    ag_s,
    ag_r,
    rs_s,
    rs_r,
    hop_s,
    hop_r,
    tok_s,
    tok_r,
    pp_s,
    pp_r,
    pb_s,
    pb_r,
):
    s = lax.axis_index("section")
    t = lax.axis_index("tensor")
    right, left, opp = lax.rem(t + 1, NT), lax.rem(t + 3, NT), lax.rem(t + 2, NT)
    nxt, prv = lax.rem(s + 1, n_sections), lax.rem(s + n_sections - 1, n_sections)
    last = n_sections - 1
    active = s < n_layers
    dim = gain.shape[1]
    qcols = qb.shape[1]
    heads = qcols // HEAD

    loads = [
        pltpu.make_async_copy(wk_hbm.at[0], w.at[:, pl.ds(0, HEAD)], w_sem.at[0]),
        pltpu.make_async_copy(wv_hbm.at[0], w.at[:, pl.ds(HEAD, HEAD)], w_sem.at[1]),
        pltpu.make_async_copy(wq_hbm.at[0], w.at[:, pl.ds(2 * HEAD, qcols)], w_sem.at[2]),
        pltpu.make_async_copy(wo_hbm.at[0], wo, w_sem.at[3]),
    ]

    def x_load(c):
        return pltpu.make_async_copy(
            flight.at[0, pl.ds(c * CR, CR)], x.at[0, c], x_sem.at[c]
        )

    def inc_load(c):
        return pltpu.make_async_copy(
            incoming.at[0, pl.ds(c * CR, CR)], x.at[1, c], inc_sem.at[c]
        )

    inc_out = pltpu.make_async_copy(incoming.at[1], out.at[0], inc_sem.at[NC])

    for c in range(NC):
        x_load(c).start()

    @pl.when(active)
    def _():
        for load in loads:
            load.start()

    @pl.when(s == 0)
    def _():
        for c in range(NC):
            inc_load(c).start()
        inc_out.start()

    bar = pltpu.get_barrier_semaphore()
    for peer in (left, right, opp):
        pl.semaphore_signal(bar, inc=1, device_id=(s, peer), device_id_type=MESH)
    pl.semaphore_signal(bar, inc=1, device_id=(prv, t), device_id_type=MESH)
    for root in (last - 1, last):

        @pl.when(s != root)
        def _():
            pl.semaphore_signal(bar, inc=1, device_id=(root, t), device_id_type=MESH)

    @pl.when(s < last - 1)
    def _():
        pl.semaphore_wait(bar, 4)

    @pl.when(s >= last - 1)
    def _():
        pl.semaphore_wait(bar, 4 + n_sections - 1)

    row8 = lax.broadcasted_iota(jnp.int32, (8, HEAD), 0)

    def token_rows(ref):
        return jnp.where(
            row8 == 0, ref[0, 0], jnp.where(row8 == 1, ref[0, 1], ref[0, 2])
        )

    tok[0] = token_rows(tokens)
    tok_copy = pltpu.make_async_remote_copy(
        tok.at[0], tok.at[1], tok_s, tok_r, device_id=(nxt, t), device_id_type=MESH
    )

    @pl.when(s != last)
    def _():
        tok_copy.start()

    @pl.when(s == 0)
    def _():
        tok[1] = token_rows(inc_tokens)

    def layout(k, b):
        n = [tok[k, p : p + 1, :] for p in range(3)]
        e0 = jnp.where(n[0] > BLOCK, 2, 1)
        e1 = e0 + jnp.where(n[1] > BLOCK, 2, 1)
        prog = jnp.where(b >= e0, 1, 0) + jnp.where(b >= e1, 1, 0)
        begin = jnp.where(prog == 0, 0, jnp.where(prog == 1, e0, e1))
        length = jnp.where(prog == 0, n[0], jnp.where(prog == 1, n[1], n[2]))
        return prog, b - begin, length

    def remote(src, dst, ssem, rsem, dev):
        return pltpu.make_async_remote_copy(
            src, dst, ssem, rsem, device_id=dev, device_id_type=MESH
        )

    def rows(ref, k, c, b, first=0, count=CR):
        return ref.at[k, c, pl.ds(pl.multiple_of(b * CR + first, HR), count)]

    def ag_send(k, c, kind):
        if kind == 0:
            r, dev = rows(g, k, c, t), (s, right)
        elif kind == 1:
            r, dev = rows(g, k, c, t), (s, left)
        elif kind == 2:
            r, dev = rows(g, k, c, left, 0, HR), (s, right)
        else:
            r, dev = rows(g, k, c, right, HR, HR), (s, left)
        return remote(r, r, ag_s.at[k, c, kind], ag_r.at[k, c, kind], dev)

    def ag_recv(k, c, kind):
        if kind == 0:
            r, dev = rows(g, k, c, left), (s, left)
        elif kind == 1:
            r, dev = rows(g, k, c, right), (s, right)
        elif kind == 2:
            r, dev = rows(g, k, c, opp, 0, HR), (s, left)
        else:
            r, dev = rows(g, k, c, opp, HR, HR), (s, right)
        return remote(r, r, ag_s.at[k, c, kind], ag_r.at[k, c, kind], dev)

    def rs_copy(k, c, kind):
        if kind == 0:
            src, dst, dev = rows(part, k, c, opp, 0, HR), ra.at[k, c], (s, left)
        elif kind == 1:
            src, dst, dev = rows(part, k, c, opp, HR, HR), rb.at[k, c], (s, right)
        elif kind == 2:
            src, dst, dev = rows(part, k, c, left, HR, HR), fr.at[k, c, pl.ds(HR, HR)], (s, left)
        elif kind == 3:
            src, dst, dev = rows(part, k, c, right, 0, HR), fl.at[k, c, pl.ds(0, HR)], (s, right)
        elif kind == 4:
            src, dst, dev = rows(part, k, c, left, 0, HR), fr.at[k, c, pl.ds(0, HR)], (s, left)
        else:
            src, dst, dev = rows(part, k, c, right, HR, HR), fl.at[k, c, pl.ds(HR, HR)], (s, right)
        return remote(src, dst, rs_s.at[k, c, kind], rs_r.at[k, c, kind], dev)

    def hop(k, c, src):
        if k == 0:
            dst = x.at[1, c]
        else:
            dst = out.at[0, pl.ds(pl.multiple_of(c * CR, CR), CR)]
        return remote(src, dst, hop_s.at[k, c], hop_r.at[k, c], (nxt, t))

    lane_row = lax.broadcasted_iota(jnp.int32, (8, HEAD), 1)

    def pool_bcast(slot, j):
        dev = (lax.rem(s + j, n_sections), t)
        return remote(pool.at[slot], pool.at[slot], pb_s.at[j], pb_r.at[slot], dev)

    def pool_parts(d):
        dev = (s, lax.rem(t + d, NT))
        return remote(pool_part.at[0], pool_part.at[d], pp_s.at[d - 1], pp_r.at[d - 1], dev)

    def pool_root(slot):
        prog, second, length = layout(0, t)
        member = (row8 == prog) & (lane_row + BLOCK * second < length)
        member = jnp.where(member, 1.0, 0.0).astype(jnp.bfloat16)
        whole = x[0].reshape(BLOCK, dim)
        pool_part[0] = jnp.dot(member, whole, preferred_element_type=jnp.float32)
        for d in range(1, NT):
            pool_parts(d).start()
        for d in range(1, NT):
            pool_parts(d).wait_recv()
        total = pool_part[0] + pool_part[1] + pool_part[2] + pool_part[3]
        count = tok[0][:, :1].astype(jnp.float32)
        mean = total / count
        emb = mean * lax.rsqrt(jnp.mean(mean * mean, axis=-1, keepdims=True) + EPS)
        pool[slot, :, 0:dim] = emb
        target = [list_rows[lists[0, p]] for p in range(3)]
        target = jnp.where(
            row8 == 0, target[0], jnp.where(row8 == 1, target[1], target[2])
        )
        target = jnp.where(row8 < 3, target, -1)
        pool[slot, :, dim : dim + HEAD] = target.astype(jnp.float32)

        def send(j, _):
            pool_bcast(slot, j).start()
            return 0

        lax.fori_loop(1, n_sections, send, 0)

    def setup(k):
        i = lax.broadcasted_iota(jnp.int32, (1, HEAD), 1)
        info = [layout(k, b) for b in range(NT)]
        for b in range(NT):
            for kb_ in range(NT):
                ok = (info[b][0] == info[kb_][0]) & (i + BLOCK * info[kb_][1] < info[kb_][2])
                mask[b : b + 1, kb_ * BLOCK : (kb_ + 1) * BLOCK] = jnp.where(ok, 0.0, NEG)
        for b in range(NT):
            second = info[b][1] > 0
            for c in range(NC):
                lo, hi = c * CR, (c + 1) * CR
                rc[c, b * CR : (b + 1) * CR] = jnp.where(
                    second, cos_tab[BLOCK + lo : BLOCK + hi], cos_tab[lo:hi]
                )
                rs[c, b * CR : (b + 1) * CR] = jnp.where(
                    second, sin_tab[BLOCK + lo : BLOCK + hi], sin_tab[lo:hi]
                )

    def ag_issue(k, c):
        v = x[k, c].astype(jnp.float32)
        scale = lax.rsqrt(jnp.mean(v * v, axis=-1, keepdims=True) + EPS)
        rows(g, k, c, t)[...] = (v * scale * gain[...]).astype(jnp.bfloat16)
        ag_send(k, c, 0).start()
        ag_send(k, c, 1).start()

    def forward(k, c):
        ag_recv(k, c, 0).wait_recv()
        ag_send(k, c, 2).start()
        ag_recv(k, c, 1).wait_recv()
        ag_send(k, c, 3).start()

    def wait_opp(k, c):
        ag_recv(k, c, 2).wait_recv()
        ag_recv(k, c, 3).wait_recv()

    def rope(v, c):
        return (v * rc[c] + pltpu.roll(v, HEAD // 2, 1) * rs[c]).astype(jnp.bfloat16)

    def qkv(k, c):
        lhs = g[k, c]
        kv = jnp.dot(lhs, w[:, 0 : 2 * HEAD], preferred_element_type=jnp.float32)
        key = rope(kv[:, :HEAD] + kb[...], c)
        val = (kv[:, HEAD:] + vb[...]).astype(jnp.bfloat16)
        for b in range(NT):
            at = pl.ds(pl.multiple_of(b * BLOCK + c * CR, CR), CR)
            k_s[at, :] = key[b * CR : (b + 1) * CR]
            v_s[at, :] = val[b * CR : (b + 1) * CR]
        for h0 in range(0, heads, 2):
            n = min(2, heads - h0)
            q = jnp.dot(
                lhs,
                w[:, (2 + h0) * HEAD : (2 + h0 + n) * HEAD],
                preferred_element_type=jnp.float32,
            )
            for j in range(n):
                h = h0 + j
                v = q[:, j * HEAD : (j + 1) * HEAD] + qb[:, h * HEAD : (h + 1) * HEAD]
                v = rope(v, c)
                for b in range(NT):
                    q_s[c, b, h * CR : (h + 1) * CR, :] = v[b * CR : (b + 1) * CR]

    def attention(c):
        scale = 1.0 / math.sqrt(HEAD)
        for b in range(NT):
            lo, hi = max(b - 1, 0) * BLOCK, min(b + 2, NT) * BLOCK
            sc = lax.dot_general(
                q_s[c, b],
                k_s[lo:hi, :],
                (((1,), (1,)), ((), ())),
                preferred_element_type=jnp.float32,
            )
            sc = sc * scale + mask[b : b + 1, lo:hi]
            e = jnp.exp(sc - jnp.max(sc, axis=-1, keepdims=True))
            p = (e * (1.0 / jnp.sum(e, axis=-1, keepdims=True))).astype(jnp.bfloat16)
            o = jnp.dot(p, v_s[lo:hi, :], preferred_element_type=jnp.float32)
            o = o.astype(jnp.bfloat16)
            for h in range(heads):
                mixed[b * CR : (b + 1) * CR, h * HEAD : (h + 1) * HEAD] = o[
                    h * CR : (h + 1) * CR
                ]

    def project(k, c):
        width = 512
        lhs = mixed[...]

        def tile(n, _):
            at = pl.ds(pl.multiple_of(n * width, width), width)
            part[k, c, :, at] = jnp.dot(
                lhs, wo[:, at], preferred_element_type=jnp.float32
            ).astype(jnp.bfloat16)
            return 0

        lax.fori_loop(0, dim // width, tile, 0)
        for kind in range(4):
            rs_copy(k, c, kind).start()

    def add_on(k, c):
        rs_copy(k, c, 0).wait_recv()
        r = rows(part, k, c, left, 0, HR)
        r[...] = (r[...].astype(jnp.float32) + ra[k, c].astype(jnp.float32)).astype(jnp.bfloat16)
        rs_copy(k, c, 4).start()
        rs_copy(k, c, 1).wait_recv()
        r = rows(part, k, c, right, HR, HR)
        r[...] = (r[...].astype(jnp.float32) + rb[k, c].astype(jnp.float32)).astype(jnp.bfloat16)
        rs_copy(k, c, 5).start()

    def finish(k, c):
        for kind in range(2, 6):
            rs_copy(k, c, kind).wait_recv()
        f32 = jnp.float32
        total = (
            rows(part, k, c, t)[...].astype(f32)
            + fl[k, c].astype(f32)
            + fr[k, c].astype(f32)
        )
        y[k, c] = (x[k, c].astype(f32) + total).astype(jnp.bfloat16)
        hop(k, c, y.at[k, c]).start()

    def wait_x1(c):
        @pl.when(s == 0)
        def _():
            inc_load(c).wait()

        @pl.when(s != 0)
        def _():
            hop(0, c, y.at[0, c]).wait_recv()

    def gather_phase(k, ahead):
        def step(c, _):
            forward(k, c)

            @pl.when(c + ahead < NC)
            def _():
                if k == 1:
                    wait_x1(c + ahead)
                ag_issue(k, c + ahead)

            @pl.when(c >= 1)
            def _():
                wait_opp(k, c - 1)
                qkv(k, c - 1)

            return 0

        lax.fori_loop(0, NC, step, 0)
        wait_opp(k, NC - 1)
        qkv(k, NC - 1)

    def reduce_phase(k):
        def step(c, _):
            attention(c)
            project(k, c)

            @pl.when(c >= 1)
            def _():
                add_on(k, c - 1)

            @pl.when(c >= 2)
            def _():
                finish(k, c - 2)

            return 0

        lax.fori_loop(0, NC, step, 0)
        add_on(k, NC - 1)
        if k == 0:
            wait_x1(0)
            ag_issue(1, 0)
        finish(k, NC - 2)
        if k == 0:
            wait_x1(1)
            ag_issue(1, 1)
        finish(k, NC - 1)

    def wait_tokens():
        @pl.when(s != 0)
        def _():
            tok_copy.wait_recv()

    @pl.when(active)
    def _():
        for c in range(2):
            x_load(c).wait()
            ag_issue(0, c)
        for c in range(2, NC):
            x_load(c).wait()
        setup(0)
        for load in loads[:3]:
            load.wait()
        gather_phase(0, 2)
        loads[3].wait()
        reduce_phase(0)
        wait_tokens()
        setup(1)
        gather_phase(1, 2)
        reduce_phase(1)

        def drain(i, _):
            c, k = lax.rem(i, NC), lax.div(i, NC)
            for kind in range(4):
                ag_send(k, c, kind).wait_send()
            for kind in range(6):
                rs_copy(k, c, kind).wait_send()
            return 0

        lax.fori_loop(0, 2 * NC, drain, 0)

    @pl.when(jnp.logical_not(active))
    def _():
        for c in range(NC):
            x_load(c).wait()

            @pl.when(s != last)
            def _():
                hop(0, c, x.at[0, c]).start()

        for slot, root in ((0, last), (1, last - 1)):

            @pl.when(s == root)
            def _():
                pool_root(slot)

        for c in range(NC):
            hop(0, c, x.at[0, c]).wait_recv()

            @pl.when(s != last)
            def _():
                hop(1, c, x.at[1, c]).start()

        wait_tokens()

        for slot, root in ((0, last), (1, last - 1)):

            @pl.when(s == root)
            def _():
                def done(j, _):
                    pool_bcast(slot, j).wait_send()
                    return 0

                lax.fori_loop(1, n_sections, done, 0)
                for d in range(1, NT):
                    pool_parts(d).wait_send()

    for slot, root in ((0, last), (1, last - 1)):

        @pl.when(s != root)
        def _():
            pool_bcast(slot, 0).wait_recv()

    own = sums.shape[0]
    mine = ((s * NT + t) * own + lax.broadcasted_iota(jnp.int32, (own, HEAD), 0)).astype(jnp.float32)
    total = jnp.zeros((own, dim), jnp.float32)
    for slot in range(2):
        for p in range(3):
            hit = mine == pool[slot, p : p + 1, dim : dim + HEAD]
            hit = jnp.where(hit, 1.0, 0.0)[:, :1]
            total = total + hit * pool[slot, p : p + 1, 0:dim]
    sums[...] = total

    @pl.when(s != last)
    def _():
        tok_copy.wait_send()
        for k in range(2):
            for c in range(NC):
                hop(k, c, y.at[k, c]).wait_send()

    @pl.when(s != 0)
    def _():
        for c in range(NC):
            hop(1, c, y.at[1, c]).wait_recv()

    @pl.when(s == 0)
    def _():
        inc_out.wait()


def solution(mesh):
    n_sections = mesh.shape["section"]
    n_layers = min(n_sections, LAYERS)
    cos_np, sin_np = rope_tables()

    def local(
        flight_state,
        flight_tokens,
        flight_lists,
        incoming,
        incoming_tokens,
        norm_gain,
        query_weight,
        query_bias,
        key_weight,
        key_bias,
        value_weight,
        value_bias,
        output_weight,
        list_rows,
    ):
        dim = flight_state.shape[-1]
        qcols = query_weight.shape[-1]
        heads = qcols // HEAD
        own = list_rows.shape[0] // (n_sections * NT)
        bf16, f32 = jnp.bfloat16, jnp.float32
        dma = pltpu.SemaphoreType.DMA
        hbm = pl.BlockSpec(memory_space=pl.ANY)
        vmem = pl.BlockSpec(memory_space=pltpu.VMEM)
        smem = pl.BlockSpec(memory_space=pltpu.SMEM)

        def body(*refs):
            kernel(n_sections, n_layers, *refs)

        return pl.pallas_call(
            body,
            out_shape=(
                jax.ShapeDtypeStruct(flight_state.shape, bf16),
                jax.ShapeDtypeStruct((own, dim), f32),
            ),
            in_specs=[
                hbm, smem, smem, hbm, smem, vmem, hbm, vmem, hbm, vmem, hbm, vmem, hbm, smem, vmem, vmem,
            ],
            out_specs=(hbm, vmem),
            scratch_shapes=[
                pltpu.VMEM((dim, qcols + 2 * HEAD), bf16),
                pltpu.VMEM((qcols, dim), bf16),
                pltpu.VMEM((2, NC, CR, dim), bf16),
                pltpu.VMEM((2, NC, CR, dim), bf16),
                pltpu.VMEM((2, NC, NT * CR, dim), bf16),
                pltpu.VMEM((2, NC, NT * CR, dim), bf16),
                pltpu.VMEM((2, NC, HR, dim), bf16),
                pltpu.VMEM((2, NC, HR, dim), bf16),
                pltpu.VMEM((2, NC, CR, dim), bf16),
                pltpu.VMEM((2, NC, CR, dim), bf16),
                pltpu.VMEM((NC, NT, heads * CR, HEAD), bf16),
                pltpu.VMEM((NT * BLOCK, HEAD), bf16),
                pltpu.VMEM((NT * BLOCK, HEAD), bf16),
                pltpu.VMEM((NT * CR, qcols), bf16),
                pltpu.VMEM((NC, NT * CR, HEAD), f32),
                pltpu.VMEM((NC, NT * CR, HEAD), f32),
                pltpu.VMEM((8, NT * BLOCK), f32),
                pltpu.VMEM((2, 8, HEAD), jnp.int32),
                pltpu.VMEM((2, 8, dim + HEAD), f32),
                pltpu.VMEM((NT, 8, dim), f32),
                dma((4,)),
                dma((NC,)),
                dma((NC + 1,)),
                dma((2, NC, 4)),
                dma((2, NC, 4)),
                dma((2, NC, 6)),
                dma((2, NC, 6)),
                dma((2, NC)),
                dma((2, NC)),
                dma,
                dma,
                dma((NT - 1,)),
                dma((NT - 1,)),
                dma((n_sections,)),
                dma((2,)),
            ],
            compiler_params=pltpu.CompilerParams(
                collective_id=0,
                has_side_effects=True,
                vmem_limit_bytes=60 * 1024 * 1024,
            ),
        )(
            flight_state,
            flight_tokens,
            flight_lists,
            incoming,
            incoming_tokens,
            norm_gain,
            query_weight,
            query_bias,
            key_weight,
            key_bias,
            value_weight,
            value_bias,
            output_weight,
            list_rows,
            jnp.asarray(cos_np),
            jnp.asarray(sin_np),
        )

    in_specs = (
        P("section", "tensor", None),
        P("section", None),
        P("section", None),
        P(None, "tensor", None),
        P(),
        P("section", None),
        P("section", None, "tensor"),
        P("section", "tensor"),
        P("section", None, "tensor"),
        P("section", "tensor"),
        P("section", None, "tensor"),
        P("section", "tensor"),
        P("section", "tensor", None),
        P(),
    )
    out_specs = (P("section", "tensor", None), P(("section", "tensor"), None))
    return jax.shard_map(local, mesh=mesh, in_specs=in_specs, out_specs=out_specs, check_vma=False)
```

```python
import math

import jax
import jax.numpy as jnp
import numpy as np
from jax import lax
from jax.experimental import pallas as pl
from jax.experimental.pallas import tpu as pltpu
from jax.sharding import PartitionSpec as P

HEAD = 128
LAYERS = 28
BLOCK = 128
EPS = 1e-06
THETA = 1000000.0

NT = 4
NC = 4
CR = BLOCK // NC
HR = CR // 2
NEG = -1e30
MESH = pl.DeviceIdType.MESH


def rope_tables():
    half = HEAD // 2
    freq = THETA ** (-np.arange(half, dtype=np.float64) * 2.0 / HEAD)
    freq = freq.astype(np.float32).astype(np.float64)
    angle = np.arange(2 * BLOCK, dtype=np.float64)[:, None] * freq[None, :]
    cosine, sine = np.cos(angle), np.sin(angle)
    return (
        np.concatenate([cosine, cosine], 1).astype(np.float32),
        np.concatenate([-sine, sine], 1).astype(np.float32),
    )


def kernel(
    n_sections,
    n_layers,
    flight,
    tokens,
    lists,
    incoming,
    inc_tokens,
    gain,
    wq_hbm,
    qb,
    wk_hbm,
    kb,
    wv_hbm,
    vb,
    wo_hbm,
    list_rows,
    cos_tab,
    sin_tab,
    out,
    sums,
    w,
    wo,
    x,
    y,
    g,
    part,
    ra,
    rb,
    fl,
    fr,
    q_s,
    k_s,
    v_s,
    mixed,
    rc,
    rs,
    mask,
    tok,
    pool,
    pool_part,
    w_sem,
    x_sem,
    inc_sem,
    ag_s,
    ag_r,
    rs_s,
    rs_r,
    hop_s,
    hop_r,
    tok_s,
    tok_r,
    pp_s,
    pp_r,
    pb_s,
    pb_r,
):
    s = lax.axis_index("section")
    t = lax.axis_index("tensor")
    right, left, opp = lax.rem(t + 1, NT), lax.rem(t + 3, NT), lax.rem(t + 2, NT)
    nxt, prv = lax.rem(s + 1, n_sections), lax.rem(s + n_sections - 1, n_sections)
    last = n_sections - 1
    active = s < n_layers
    dim = gain.shape[1]
    qcols = qb.shape[1]
    heads = qcols // HEAD

    def rows(ref, k, c, b, first=0, count=CR):
        return ref.at[k, c, pl.ds(pl.multiple_of(b * CR + first, HR), count)]

    def norm(k, c):
        v = x[k, c].astype(jnp.float32)
        scale = lax.rsqrt(jnp.mean(v * v, axis=-1, keepdims=True) + EPS)
        rows(g, k, c, t)[...] = (v * scale * gain[...]).astype(jnp.bfloat16)

    loads = [
        pltpu.make_async_copy(wk_hbm.at[0], w.at[:, pl.ds(0, HEAD)], w_sem.at[0]),
        pltpu.make_async_copy(wv_hbm.at[0], w.at[:, pl.ds(HEAD, HEAD)], w_sem.at[1]),
        pltpu.make_async_copy(wq_hbm.at[0], w.at[:, pl.ds(2 * HEAD, qcols)], w_sem.at[2]),
        pltpu.make_async_copy(wo_hbm.at[0], wo, w_sem.at[3]),
    ]

    def x_load(c):
        return pltpu.make_async_copy(
            flight.at[0, pl.ds(c * CR, CR)], x.at[0, c], x_sem.at[c]
        )

    def inc_load(c):
        return pltpu.make_async_copy(
            incoming.at[0, pl.ds(c * CR, CR)], x.at[1, c], inc_sem.at[c]
        )

    inc_out = pltpu.make_async_copy(incoming.at[1], out.at[0], inc_sem.at[NC])

    for c in range(NC):
        x_load(c).start()

    @pl.when(active)
    def _():
        for load in loads:
            load.start()

    @pl.when(s == 0)
    def _():
        for c in range(NC):
            inc_load(c).start()
        inc_out.start()

    bar = pltpu.get_barrier_semaphore()
    for peer in (left, right, opp):
        pl.semaphore_signal(bar, inc=1, device_id=(s, peer), device_id_type=MESH)
    pl.semaphore_signal(bar, inc=1, device_id=(prv, t), device_id_type=MESH)
    for root in (last - 1, last):

        @pl.when(s != root)
        def _():
            pl.semaphore_signal(bar, inc=1, device_id=(root, t), device_id_type=MESH)

    for c in range(NC):
        x_load(c).wait()

    @pl.when(active)
    def _():
        for c in range(NC):
            norm(0, c)

    @pl.when(s < last - 1)
    def _():
        pl.semaphore_wait(bar, 4)

    @pl.when(s >= last - 1)
    def _():
        pl.semaphore_wait(bar, 4 + n_sections - 1)

    row8 = lax.broadcasted_iota(jnp.int32, (8, HEAD), 0)

    def token_rows(ref):
        return jnp.where(
            row8 == 0, ref[0, 0], jnp.where(row8 == 1, ref[0, 1], ref[0, 2])
        )

    tok[0] = token_rows(tokens)
    tok_copy = pltpu.make_async_remote_copy(
        tok.at[0], tok.at[1], tok_s, tok_r, device_id=(nxt, t), device_id_type=MESH
    )

    @pl.when(s != last)
    def _():
        tok_copy.start()

    @pl.when(s == 0)
    def _():
        tok[1] = token_rows(inc_tokens)

    def layout(k, b):
        n = [tok[k, p : p + 1, :] for p in range(3)]
        e0 = jnp.where(n[0] > BLOCK, 2, 1)
        e1 = e0 + jnp.where(n[1] > BLOCK, 2, 1)
        prog = jnp.where(b >= e0, 1, 0) + jnp.where(b >= e1, 1, 0)
        begin = jnp.where(prog == 0, 0, jnp.where(prog == 1, e0, e1))
        length = jnp.where(prog == 0, n[0], jnp.where(prog == 1, n[1], n[2]))
        return prog, b - begin, length

    def remote(src, dst, ssem, rsem, dev):
        return pltpu.make_async_remote_copy(
            src, dst, ssem, rsem, device_id=dev, device_id_type=MESH
        )

    def ag_send(k, c, kind):
        if kind == 0:
            r, dev = rows(g, k, c, t), (s, right)
        elif kind == 1:
            r, dev = rows(g, k, c, t), (s, left)
        elif kind == 2:
            r, dev = rows(g, k, c, left, 0, HR), (s, right)
        else:
            r, dev = rows(g, k, c, right, HR, HR), (s, left)
        return remote(r, r, ag_s.at[k, c, kind], ag_r.at[k, c, kind], dev)

    def ag_recv(k, c, kind):
        if kind == 0:
            r, dev = rows(g, k, c, left), (s, left)
        elif kind == 1:
            r, dev = rows(g, k, c, right), (s, right)
        elif kind == 2:
            r, dev = rows(g, k, c, opp, 0, HR), (s, left)
        else:
            r, dev = rows(g, k, c, opp, HR, HR), (s, right)
        return remote(r, r, ag_s.at[k, c, kind], ag_r.at[k, c, kind], dev)

    def rs_copy(k, c, kind):
        if kind == 0:
            src, dst, dev = rows(part, k, c, opp, 0, HR), ra.at[k, c], (s, left)
        elif kind == 1:
            src, dst, dev = rows(part, k, c, opp, HR, HR), rb.at[k, c], (s, right)
        elif kind == 2:
            src, dst, dev = rows(part, k, c, left, HR, HR), fr.at[k, c, pl.ds(HR, HR)], (s, left)
        elif kind == 3:
            src, dst, dev = rows(part, k, c, right, 0, HR), fl.at[k, c, pl.ds(0, HR)], (s, right)
        elif kind == 4:
            src, dst, dev = rows(part, k, c, left, 0, HR), fr.at[k, c, pl.ds(0, HR)], (s, left)
        else:
            src, dst, dev = rows(part, k, c, right, HR, HR), fl.at[k, c, pl.ds(HR, HR)], (s, right)
        return remote(src, dst, rs_s.at[k, c, kind], rs_r.at[k, c, kind], dev)

    def hop(k, c, half, src):
        if k == 0:
            dst = x.at[1, c, pl.ds(half * HR, HR)]
        else:
            dst = out.at[0, pl.ds(pl.multiple_of(c * CR + half * HR, HR), HR)]
        src = src.at[k, c, pl.ds(half * HR, HR)]
        return remote(src, dst, hop_s.at[k, c, half], hop_r.at[k, c, half], (nxt, t))

    lane_row = lax.broadcasted_iota(jnp.int32, (8, HEAD), 1)

    def pool_bcast(slot, j):
        dev = (lax.rem(s + j, n_sections), t)
        return remote(pool.at[slot], pool.at[slot], pb_s.at[j], pb_r.at[slot], dev)

    def pool_parts(d):
        dev = (s, lax.rem(t + d, NT))
        return remote(pool_part.at[0], pool_part.at[d], pp_s.at[d - 1], pp_r.at[d - 1], dev)

    def pool_root(slot):
        prog, second, length = layout(0, t)
        member = (row8 == prog) & (lane_row + BLOCK * second < length)
        member = jnp.where(member, 1.0, 0.0).astype(jnp.bfloat16)
        whole = x[0].reshape(BLOCK, dim)
        pool_part[0] = jnp.dot(member, whole, preferred_element_type=jnp.float32)
        for d in range(1, NT):
            pool_parts(d).start()
        for d in range(1, NT):
            pool_parts(d).wait_recv()
        total = pool_part[0] + pool_part[1] + pool_part[2] + pool_part[3]
        count = tok[0][:, :1].astype(jnp.float32)
        mean = total / count
        emb = mean * lax.rsqrt(jnp.mean(mean * mean, axis=-1, keepdims=True) + EPS)
        pool[slot, :, 0:dim] = emb
        target = [list_rows[lists[0, p]] for p in range(3)]
        target = jnp.where(
            row8 == 0, target[0], jnp.where(row8 == 1, target[1], target[2])
        )
        target = jnp.where(row8 < 3, target, -1)
        pool[slot, :, dim : dim + HEAD] = target.astype(jnp.float32)

        def send(j, _):
            pool_bcast(slot, j).start()
            return 0

        lax.fori_loop(1, n_sections, send, 0)

    def setup(k):
        i = lax.broadcasted_iota(jnp.int32, (1, HEAD), 1)
        info = [layout(k, b) for b in range(NT)]
        for b in range(NT):
            for kb_ in range(NT):
                ok = (info[b][0] == info[kb_][0]) & (i + BLOCK * info[kb_][1] < info[kb_][2])
                mask[b : b + 1, kb_ * BLOCK : (kb_ + 1) * BLOCK] = jnp.where(ok, 0.0, NEG)
        for b in range(NT):
            second = info[b][1] > 0
            for c in range(NC):
                lo, hi = c * CR, (c + 1) * CR
                rc[c, b * CR : (b + 1) * CR] = jnp.where(
                    second, cos_tab[BLOCK + lo : BLOCK + hi], cos_tab[lo:hi]
                )
                rs[c, b * CR : (b + 1) * CR] = jnp.where(
                    second, sin_tab[BLOCK + lo : BLOCK + hi], sin_tab[lo:hi]
                )

    def ag_start(k, c):
        ag_send(k, c, 0).start()
        ag_send(k, c, 1).start()

    def forward(k, c):
        ag_recv(k, c, 0).wait_recv()
        ag_send(k, c, 2).start()
        ag_recv(k, c, 1).wait_recv()
        ag_send(k, c, 3).start()

    def wait_opp(k, c):
        ag_recv(k, c, 2).wait_recv()
        ag_recv(k, c, 3).wait_recv()

    def rope(v, c):
        return (v * rc[c] + pltpu.roll(v, HEAD // 2, 1) * rs[c]).astype(jnp.bfloat16)

    def keys_values(k, c):
        kv = jnp.dot(g[k, c], w[:, 0 : 2 * HEAD], preferred_element_type=jnp.float32)
        key = rope(kv[:, :HEAD] + kb[...], c)
        val = (kv[:, HEAD:] + vb[...]).astype(jnp.bfloat16)
        for b in range(NT):
            at = pl.ds(pl.multiple_of(b * BLOCK + c * CR, CR), CR)
            k_s[at, :] = key[b * CR : (b + 1) * CR]
            v_s[at, :] = val[b * CR : (b + 1) * CR]

    def queries(k, c):
        lhs = g[k, c]
        for h0 in range(0, heads, 2):
            n = min(2, heads - h0)
            q = jnp.dot(
                lhs,
                w[:, (2 + h0) * HEAD : (2 + h0 + n) * HEAD],
                preferred_element_type=jnp.float32,
            )
            for j in range(n):
                h = h0 + j
                v = q[:, j * HEAD : (j + 1) * HEAD] + qb[:, h * HEAD : (h + 1) * HEAD]
                v = rope(v, c)
                for b in range(NT):
                    q_s[c, b, h * CR : (h + 1) * CR, :] = v[b * CR : (b + 1) * CR]

    def attention(c):
        scale = 1.0 / math.sqrt(HEAD)
        spans = [(max(b - 1, 0) * BLOCK, min(b + 2, NT) * BLOCK) for b in range(NT)]
        scores = [
            lax.dot_general(
                q_s[c, b],
                k_s[lo:hi, :],
                (((1,), (1,)), ((), ())),
                preferred_element_type=jnp.float32,
            )
            for b, (lo, hi) in enumerate(spans)
        ]
        outs = []
        for b, (lo, hi) in enumerate(spans):
            sc = scores[b] * scale + mask[b : b + 1, lo:hi]
            e = jnp.exp(sc - jnp.max(sc, axis=-1, keepdims=True))
            p = (e * (1.0 / jnp.sum(e, axis=-1, keepdims=True))).astype(jnp.bfloat16)
            o = jnp.dot(p, v_s[lo:hi, :], preferred_element_type=jnp.float32)
            outs.append(o.astype(jnp.bfloat16))
        for b in range(NT):
            for h in range(heads):
                mixed[b * CR : (b + 1) * CR, h * HEAD : (h + 1) * HEAD] = outs[b][
                    h * CR : (h + 1) * CR
                ]

    def project(k, c):
        width = 512
        lhs = mixed[...]
        for n in range(0, dim, width):
            part[k, c, :, n : n + width] = jnp.dot(
                lhs, wo[:, n : n + width], preferred_element_type=jnp.float32
            ).astype(jnp.bfloat16)
        for kind in range(4):
            rs_copy(k, c, kind).start()

    def add_on(k, c):
        rs_copy(k, c, 0).wait_recv()
        r = rows(part, k, c, left, 0, HR)
        r[...] = (r[...].astype(jnp.float32) + ra[k, c].astype(jnp.float32)).astype(jnp.bfloat16)
        rs_copy(k, c, 4).start()
        rs_copy(k, c, 1).wait_recv()
        r = rows(part, k, c, right, HR, HR)
        r[...] = (r[...].astype(jnp.float32) + rb[k, c].astype(jnp.float32)).astype(jnp.bfloat16)
        rs_copy(k, c, 5).start()

    def finish(k, c):
        f32 = jnp.float32
        for half, kinds in ((0, (3, 4)), (1, (2, 5))):
            for kind in kinds:
                rs_copy(k, c, kind).wait_recv()
            at = pl.ds(half * HR, HR)
            total = (
                rows(part, k, c, t, half * HR, HR)[...].astype(f32)
                + fl[k, c, at].astype(f32)
                + fr[k, c, at].astype(f32)
            )
            y[k, c, at] = (x[k, c, at].astype(f32) + total).astype(jnp.bfloat16)
            hop(k, c, half, y).start()

    def wait_x1(c):
        @pl.when(s == 0)
        def _():
            inc_load(c).wait()

        @pl.when(s != 0)
        def _():
            for half in range(2):
                hop(0, c, half, y).wait_recv()

    def first(c):
        wait_x1(c)
        norm(1, c)
        ag_start(1, c)

    def gather_phase(k, ahead):
        def step(c, _):
            forward(k, c)

            @pl.when(c + ahead < NC)
            def _():
                if k == 1:
                    wait_x1(c + ahead)
                    norm(k, c + ahead)
                ag_start(k, c + ahead)

            @pl.when(c >= 1)
            def _():
                wait_opp(k, c - 1)
                keys_values(k, c - 1)
                queries(k, c - 1)

            return 0

        lax.fori_loop(0, NC, step, 0)
        wait_opp(k, NC - 1)
        keys_values(k, NC - 1)

    def reduce_phase(k):
        def step(c, _):
            attention(c)
            project(k, c)

            @pl.when(c == 0)
            def _():
                queries(k, NC - 1)

            @pl.when(c >= 1)
            def _():
                add_on(k, c - 1)

            @pl.when(c >= 2)
            def _():
                finish(k, c - 2)

            return 0

        lax.fori_loop(0, NC, step, 0)
        if k == 0:
            first(0)
        add_on(k, NC - 1)
        finish(k, NC - 2)
        if k == 0:
            first(1)
        finish(k, NC - 1)

    def wait_tokens():
        @pl.when(s != 0)
        def _():
            tok_copy.wait_recv()

    @pl.when(active)
    def _():
        ag_start(0, 0)
        ag_start(0, 1)
        setup(0)
        for load in loads[:3]:
            load.wait()
        gather_phase(0, 2)
        loads[3].wait()
        reduce_phase(0)
        wait_tokens()
        setup(1)
        gather_phase(1, 2)
        reduce_phase(1)

        def drain(i, _):
            c, k = lax.rem(i, NC), lax.div(i, NC)
            for kind in range(4):
                ag_send(k, c, kind).wait_send()
            for kind in range(6):
                rs_copy(k, c, kind).wait_send()
            return 0

        lax.fori_loop(0, 2 * NC, drain, 0)

    @pl.when(jnp.logical_not(active))
    def _():
        for c in range(NC):

            @pl.when(s != last)
            def _():
                for half in range(2):
                    hop(0, c, half, x).start()

        for slot, root in ((0, last), (1, last - 1)):

            @pl.when(s == root)
            def _():
                pool_root(slot)

        for c in range(NC):
            for half in range(2):
                hop(0, c, half, x).wait_recv()

            @pl.when(s != last)
            def _():
                for half in range(2):
                    hop(1, c, half, x).start()

        wait_tokens()

        for slot, root in ((0, last), (1, last - 1)):

            @pl.when(s == root)
            def _():
                def done(j, _):
                    pool_bcast(slot, j).wait_send()
                    return 0

                lax.fori_loop(1, n_sections, done, 0)
                for d in range(1, NT):
                    pool_parts(d).wait_send()

    for slot, root in ((0, last), (1, last - 1)):

        @pl.when(s != root)
        def _():
            pool_bcast(slot, 0).wait_recv()

    own = sums.shape[0]
    mine = ((s * NT + t) * own + lax.broadcasted_iota(jnp.int32, (own, HEAD), 0)).astype(jnp.float32)
    total = jnp.zeros((own, dim), jnp.float32)
    for slot in range(2):
        for p in range(3):
            hit = mine == pool[slot, p : p + 1, dim : dim + HEAD]
            hit = jnp.where(hit, 1.0, 0.0)[:, :1]
            total = total + hit * pool[slot, p : p + 1, 0:dim]
    sums[...] = total

    @pl.when(s != last)
    def _():
        tok_copy.wait_send()
        for k in range(2):
            for c in range(NC):
                for half in range(2):
                    hop(k, c, half, y).wait_send()

    @pl.when(s != 0)
    def _():
        for c in range(NC):
            for half in range(2):
                hop(1, c, half, y).wait_recv()

    @pl.when(s == 0)
    def _():
        inc_out.wait()


def solution(mesh):
    n_sections = mesh.shape["section"]
    n_layers = min(n_sections, LAYERS)
    cos_np, sin_np = rope_tables()

    def local(
        flight_state,
        flight_tokens,
        flight_lists,
        incoming,
        incoming_tokens,
        norm_gain,
        query_weight,
        query_bias,
        key_weight,
        key_bias,
        value_weight,
        value_bias,
        output_weight,
        list_rows,
    ):
        dim = flight_state.shape[-1]
        qcols = query_weight.shape[-1]
        heads = qcols // HEAD
        own = list_rows.shape[0] // (n_sections * NT)
        bf16, f32 = jnp.bfloat16, jnp.float32
        dma = pltpu.SemaphoreType.DMA
        hbm = pl.BlockSpec(memory_space=pl.ANY)
        vmem = pl.BlockSpec(memory_space=pltpu.VMEM)
        smem = pl.BlockSpec(memory_space=pltpu.SMEM)

        def body(*refs):
            kernel(n_sections, n_layers, *refs)

        return pl.pallas_call(
            body,
            out_shape=(
                jax.ShapeDtypeStruct(flight_state.shape, bf16),
                jax.ShapeDtypeStruct((own, dim), f32),
            ),
            in_specs=[
                hbm, smem, smem, hbm, smem, vmem, hbm, vmem, hbm, vmem, hbm, vmem, hbm, smem, vmem, vmem,
            ],
            out_specs=(hbm, vmem),
            scratch_shapes=[
                pltpu.VMEM((dim, qcols + 2 * HEAD), bf16),
                pltpu.VMEM((qcols, dim), bf16),
                pltpu.VMEM((2, NC, CR, dim), bf16),
                pltpu.VMEM((2, NC, CR, dim), bf16),
                pltpu.VMEM((2, NC, NT * CR, dim), bf16),
                pltpu.VMEM((2, NC, NT * CR, dim), bf16),
                pltpu.VMEM((2, NC, HR, dim), bf16),
                pltpu.VMEM((2, NC, HR, dim), bf16),
                pltpu.VMEM((2, NC, CR, dim), bf16),
                pltpu.VMEM((2, NC, CR, dim), bf16),
                pltpu.VMEM((NC, NT, heads * CR, HEAD), bf16),
                pltpu.VMEM((NT * BLOCK, HEAD), bf16),
                pltpu.VMEM((NT * BLOCK, HEAD), bf16),
                pltpu.VMEM((NT * CR, qcols), bf16),
                pltpu.VMEM((NC, NT * CR, HEAD), f32),
                pltpu.VMEM((NC, NT * CR, HEAD), f32),
                pltpu.VMEM((8, NT * BLOCK), f32),
                pltpu.VMEM((2, 8, HEAD), jnp.int32),
                pltpu.VMEM((2, 8, dim + HEAD), f32),
                pltpu.VMEM((NT, 8, dim), f32),
                dma((4,)),
                dma((NC,)),
                dma((NC + 1,)),
                dma((2, NC, 4)),
                dma((2, NC, 4)),
                dma((2, NC, 6)),
                dma((2, NC, 6)),
                dma((2, NC, 2)),
                dma((2, NC, 2)),
                dma,
                dma,
                dma((NT - 1,)),
                dma((NT - 1,)),
                dma((n_sections,)),
                dma((2,)),
            ],
            compiler_params=pltpu.CompilerParams(
                collective_id=0,
                has_side_effects=True,
                vmem_limit_bytes=60 * 1024 * 1024,
            ),
        )(
            flight_state,
            flight_tokens,
            flight_lists,
            incoming,
            incoming_tokens,
            norm_gain,
            query_weight,
            query_bias,
            key_weight,
            key_bias,
            value_weight,
            value_bias,
            output_weight,
            list_rows,
            jnp.asarray(cos_np),
            jnp.asarray(sin_np),
        )

    in_specs = (
        P("section", "tensor", None),
        P("section", None),
        P("section", None),
        P(None, "tensor", None),
        P(),
        P("section", None),
        P("section", None, "tensor"),
        P("section", "tensor"),
        P("section", None, "tensor"),
        P("section", "tensor"),
        P("section", None, "tensor"),
        P("section", "tensor"),
        P("section", "tensor", None),
        P(),
    )
    out_specs = (P("section", "tensor", None), P(("section", "tensor"), None))
    return jax.shard_map(local, mesh=mesh, in_specs=in_specs, out_specs=out_specs, check_vma=False)
```

```python
import math

import jax
import jax.numpy as jnp
import numpy as np
from jax import lax
from jax.experimental import pallas as pl
from jax.experimental.pallas import tpu as pltpu
from jax.sharding import PartitionSpec as P

HEAD = 128
LAYERS = 28
BLOCK = 128
EPS = 1e-06
THETA = 1000000.0

NT = 4
NC = 4
CR = BLOCK // NC
HR = CR // 2
NEG = -1e30
MESH = pl.DeviceIdType.MESH


def rope_tables():
    half = HEAD // 2
    freq = THETA ** (-np.arange(half, dtype=np.float64) * 2.0 / HEAD)
    freq = freq.astype(np.float32).astype(np.float64)
    angle = np.arange(2 * BLOCK, dtype=np.float64)[:, None] * freq[None, :]
    cosine, sine = np.cos(angle), np.sin(angle)
    return (
        np.concatenate([cosine, cosine], 1).astype(np.float32),
        np.concatenate([-sine, sine], 1).astype(np.float32),
    )


def kernel(
    n_sections,
    n_layers,
    flight,
    tokens,
    lists,
    incoming,
    inc_tokens,
    gain,
    wq_hbm,
    qb,
    wk_hbm,
    kb,
    wv_hbm,
    vb,
    wo_hbm,
    list_rows,
    cos_hbm,
    sin_hbm,
    out,
    sums,
    w,
    wo,
    x,
    y,
    g,
    part,
    ra,
    rb,
    fl,
    fr,
    q_s,
    k_s,
    v_s,
    mixed,
    rc,
    rs,
    mask,
    tok,
    pool,
    pool_part,
    w_sem,
    x_sem,
    inc_sem,
    ag_s,
    ag_r,
    rs_s,
    rs_r,
    hop_s,
    hop_r,
    tok_s,
    tok_r,
    pp_s,
    pp_r,
    pb_s,
    pb_r,
    sum_buf,
    sum_sem,
    cos_tab,
    sin_tab,
    tab_sem,
):
    s = lax.axis_index("section")
    t = lax.axis_index("tensor")
    right, left, opp = lax.rem(t + 1, NT), lax.rem(t + 3, NT), lax.rem(t + 2, NT)
    nxt, prv = lax.rem(s + 1, n_sections), lax.rem(s + n_sections - 1, n_sections)
    last = n_sections - 1
    active = s < n_layers
    dim = gain.shape[1]
    qcols = qb.shape[1]
    heads = qcols // HEAD

    def rows(ref, k, c, b, first=0, count=CR):
        return ref.at[k, c, pl.ds(pl.multiple_of(b * CR + first, HR), count)]

    def norm(k, c):
        v = x[k, c].astype(jnp.float32)
        scale = lax.rsqrt(jnp.mean(v * v, axis=-1, keepdims=True) + EPS)
        rows(g, k, c, t)[...] = (v * scale * gain[...]).astype(jnp.bfloat16)

    loads = [
        pltpu.make_async_copy(wk_hbm.at[0], w.at[:, pl.ds(0, HEAD)], w_sem.at[0]),
        pltpu.make_async_copy(wv_hbm.at[0], w.at[:, pl.ds(HEAD, HEAD)], w_sem.at[1]),
        pltpu.make_async_copy(wq_hbm.at[0], w.at[:, pl.ds(2 * HEAD, qcols)], w_sem.at[2]),
        pltpu.make_async_copy(wo_hbm.at[0], wo, w_sem.at[3]),
    ]

    tables = [
        pltpu.make_async_copy(cos_hbm, cos_tab, tab_sem.at[0]),
        pltpu.make_async_copy(sin_hbm, sin_tab, tab_sem.at[1]),
    ]

    def x_load(c):
        return pltpu.make_async_copy(
            flight.at[0, pl.ds(c * CR, CR)], x.at[0, c], x_sem.at[c]
        )

    def inc_load(c):
        return pltpu.make_async_copy(
            incoming.at[0, pl.ds(c * CR, CR)], x.at[1, c], inc_sem.at[c]
        )

    inc_out = pltpu.make_async_copy(incoming.at[1], out.at[0], inc_sem.at[NC])

    for c in range(NC):
        x_load(c).start()

    @pl.when(active)
    def _():
        for load in tables + loads:
            load.start()

    @pl.when(s == 0)
    def _():
        for c in range(NC):
            inc_load(c).start()
        inc_out.start()

    bar = pltpu.get_barrier_semaphore()
    for peer in (left, right, opp):
        pl.semaphore_signal(bar, inc=1, device_id=(s, peer), device_id_type=MESH)
    pl.semaphore_signal(bar, inc=1, device_id=(prv, t), device_id_type=MESH)
    for root in (last - 1, last):

        @pl.when(s != root)
        def _():
            pl.semaphore_signal(bar, inc=1, device_id=(root, t), device_id_type=MESH)

    for c in range(NC):
        x_load(c).wait()

    @pl.when(active)
    def _():
        for c in range(NC):
            norm(0, c)

    @pl.when(s < last - 1)
    def _():
        pl.semaphore_wait(bar, 4)

    @pl.when(s >= last - 1)
    def _():
        pl.semaphore_wait(bar, 4 + n_sections - 1)

    row8 = lax.broadcasted_iota(jnp.int32, (8, HEAD), 0)

    def token_rows(ref):
        return jnp.where(
            row8 == 0, ref[0, 0], jnp.where(row8 == 1, ref[0, 1], ref[0, 2])
        )

    tok[0] = token_rows(tokens)
    tok_copy = pltpu.make_async_remote_copy(
        tok.at[0], tok.at[1], tok_s, tok_r, device_id=(nxt, t), device_id_type=MESH
    )

    @pl.when(s != last)
    def _():
        tok_copy.start()

    @pl.when(s == 0)
    def _():
        tok[1] = token_rows(inc_tokens)

    def layout(k, b):
        n = [tok[k, p : p + 1, :] for p in range(3)]
        e0 = jnp.where(n[0] > BLOCK, 2, 1)
        e1 = e0 + jnp.where(n[1] > BLOCK, 2, 1)
        prog = jnp.where(b >= e0, 1, 0) + jnp.where(b >= e1, 1, 0)
        begin = jnp.where(prog == 0, 0, jnp.where(prog == 1, e0, e1))
        length = jnp.where(prog == 0, n[0], jnp.where(prog == 1, n[1], n[2]))
        return prog, b - begin, length

    def remote(src, dst, ssem, rsem, dev):
        return pltpu.make_async_remote_copy(
            src, dst, ssem, rsem, device_id=dev, device_id_type=MESH
        )

    def ag_send(k, c, kind):
        if kind == 0:
            r, dev = rows(g, k, c, t), (s, right)
        elif kind == 1:
            r, dev = rows(g, k, c, t), (s, left)
        elif kind == 2:
            r, dev = rows(g, k, c, left, 0, HR), (s, right)
        else:
            r, dev = rows(g, k, c, right, HR, HR), (s, left)
        return remote(r, r, ag_s.at[k, c, kind], ag_r.at[k, c, kind], dev)

    def ag_recv(k, c, kind):
        if kind == 0:
            r, dev = rows(g, k, c, left), (s, left)
        elif kind == 1:
            r, dev = rows(g, k, c, right), (s, right)
        elif kind == 2:
            r, dev = rows(g, k, c, opp, 0, HR), (s, left)
        else:
            r, dev = rows(g, k, c, opp, HR, HR), (s, right)
        return remote(r, r, ag_s.at[k, c, kind], ag_r.at[k, c, kind], dev)

    def rs_copy(k, c, kind):
        if kind == 0:
            src, dst, dev = rows(part, k, c, opp, 0, HR), ra.at[k, c], (s, left)
        elif kind == 1:
            src, dst, dev = rows(part, k, c, opp, HR, HR), rb.at[k, c], (s, right)
        elif kind == 2:
            src, dst, dev = rows(part, k, c, left, HR, HR), fr.at[k, c, pl.ds(HR, HR)], (s, left)
        elif kind == 3:
            src, dst, dev = rows(part, k, c, right, 0, HR), fl.at[k, c, pl.ds(0, HR)], (s, right)
        elif kind == 4:
            src, dst, dev = rows(part, k, c, left, 0, HR), fr.at[k, c, pl.ds(0, HR)], (s, left)
        else:
            src, dst, dev = rows(part, k, c, right, HR, HR), fl.at[k, c, pl.ds(HR, HR)], (s, right)
        return remote(src, dst, rs_s.at[k, c, kind], rs_r.at[k, c, kind], dev)

    def hop(k, c, half, src):
        if k == 0:
            dst = x.at[1, c, pl.ds(half * HR, HR)]
        else:
            dst = out.at[0, pl.ds(pl.multiple_of(c * CR + half * HR, HR), HR)]
        src = src.at[k, c, pl.ds(half * HR, HR)]
        return remote(src, dst, hop_s.at[k, c, half], hop_r.at[k, c, half], (nxt, t))

    lane_row = lax.broadcasted_iota(jnp.int32, (8, HEAD), 1)

    def pool_bcast(slot, j):
        dev = (lax.rem(s + j, n_sections), t)
        return remote(pool.at[slot], pool.at[slot], pb_s.at[j], pb_r.at[slot], dev)

    def pool_parts(d):
        dev = (s, lax.rem(t + d, NT))
        return remote(pool_part.at[0], pool_part.at[d], pp_s.at[d - 1], pp_r.at[d - 1], dev)

    def pool_root(slot):
        prog, second, length = layout(0, t)
        member = (row8 == prog) & (lane_row + BLOCK * second < length)
        member = jnp.where(member, 1.0, 0.0).astype(jnp.bfloat16)
        whole = x[0].reshape(BLOCK, dim)
        pool_part[0] = jnp.dot(member, whole, preferred_element_type=jnp.float32)
        for d in range(1, NT):
            pool_parts(d).start()
        for d in range(1, NT):
            pool_parts(d).wait_recv()
        total = pool_part[0] + pool_part[1] + pool_part[2] + pool_part[3]
        count = tok[0][:, :1].astype(jnp.float32)
        mean = total / count
        emb = mean * lax.rsqrt(jnp.mean(mean * mean, axis=-1, keepdims=True) + EPS)
        pool[slot, :, 0:dim] = emb
        target = [list_rows[lists[0, p]] for p in range(3)]
        target = jnp.where(
            row8 == 0, target[0], jnp.where(row8 == 1, target[1], target[2])
        )
        target = jnp.where(row8 < 3, target, -1)
        pool[slot, :, dim : dim + HEAD] = target.astype(jnp.float32)

        def send(j, _):
            pool_bcast(slot, j).start()
            return 0

        lax.fori_loop(1, n_sections, send, 0)

    def setup(k):
        i = lax.broadcasted_iota(jnp.int32, (1, HEAD), 1)
        info = [layout(k, b) for b in range(NT)]
        for b in range(NT):
            for kb_ in range(NT):
                ok = (info[b][0] == info[kb_][0]) & (i + BLOCK * info[kb_][1] < info[kb_][2])
                mask[k, b : b + 1, kb_ * BLOCK : (kb_ + 1) * BLOCK] = jnp.where(ok, 0.0, NEG)
        for b in range(NT):
            second = info[b][1] > 0
            for c in range(NC):
                lo, hi = c * CR, (c + 1) * CR
                rc[k, c, b * CR : (b + 1) * CR] = jnp.where(
                    second, cos_tab[BLOCK + lo : BLOCK + hi], cos_tab[lo:hi]
                )
                rs[k, c, b * CR : (b + 1) * CR] = jnp.where(
                    second, sin_tab[BLOCK + lo : BLOCK + hi], sin_tab[lo:hi]
                )

    def ag_start(k, c):
        ag_send(k, c, 0).start()
        ag_send(k, c, 1).start()

    def forward(k, c):
        ag_recv(k, c, 0).wait_recv()
        ag_send(k, c, 2).start()
        ag_recv(k, c, 1).wait_recv()
        ag_send(k, c, 3).start()

    def wait_opp(k, c):
        ag_recv(k, c, 2).wait_recv()
        ag_recv(k, c, 3).wait_recv()

    def rope(v, k, c):
        return (v * rc[k, c] + pltpu.roll(v, HEAD // 2, 1) * rs[k, c]).astype(jnp.bfloat16)

    def keys_values(k, c):
        kv = jnp.dot(g[k, c], w[:, 0 : 2 * HEAD], preferred_element_type=jnp.float32)
        key = rope(kv[:, :HEAD] + kb[...], k, c)
        val = (kv[:, HEAD:] + vb[...]).astype(jnp.bfloat16)
        for b in range(NT):
            at = pl.ds(pl.multiple_of(b * BLOCK + c * CR, CR), CR)
            k_s[at, :] = key[b * CR : (b + 1) * CR]
            v_s[at, :] = val[b * CR : (b + 1) * CR]

    def queries(k, c):
        lhs = g[k, c]
        for h0 in range(0, heads, 2):
            n = min(2, heads - h0)
            q = jnp.dot(
                lhs,
                w[:, (2 + h0) * HEAD : (2 + h0 + n) * HEAD],
                preferred_element_type=jnp.float32,
            )
            for j in range(n):
                h = h0 + j
                v = q[:, j * HEAD : (j + 1) * HEAD] + qb[:, h * HEAD : (h + 1) * HEAD]
                v = rope(v, k, c)
                for b in range(NT):
                    q_s[c, b, h * CR : (h + 1) * CR, :] = v[b * CR : (b + 1) * CR]

    def attention(k, c):
        scale = 1.0 / math.sqrt(HEAD)
        spans = [(max(b - 1, 0) * BLOCK, min(b + 2, NT) * BLOCK) for b in range(NT)]
        scores = [
            lax.dot_general(
                q_s[c, b],
                k_s[lo:hi, :],
                (((1,), (1,)), ((), ())),
                preferred_element_type=jnp.float32,
            )
            for b, (lo, hi) in enumerate(spans)
        ]
        outs = []
        for b, (lo, hi) in enumerate(spans):
            sc = scores[b] * scale + mask[k, b : b + 1, lo:hi]
            e = jnp.exp(sc - jnp.max(sc, axis=-1, keepdims=True))
            p = (e * (1.0 / jnp.sum(e, axis=-1, keepdims=True))).astype(jnp.bfloat16)
            o = jnp.dot(p, v_s[lo:hi, :], preferred_element_type=jnp.float32)
            outs.append(o.astype(jnp.bfloat16))
        for b in range(NT):
            for h in range(heads):
                mixed[b * CR : (b + 1) * CR, h * HEAD : (h + 1) * HEAD] = outs[b][
                    h * CR : (h + 1) * CR
                ]

    def project(k, c):
        width = 512
        lhs = mixed[...]
        for n in range(0, dim, width):
            part[k, c, :, n : n + width] = jnp.dot(
                lhs, wo[:, n : n + width], preferred_element_type=jnp.float32
            ).astype(jnp.bfloat16)
        for kind in range(4):
            rs_copy(k, c, kind).start()

    def add_on(k, c):
        rs_copy(k, c, 0).wait_recv()
        r = rows(part, k, c, left, 0, HR)
        r[...] = (r[...].astype(jnp.float32) + ra[k, c].astype(jnp.float32)).astype(jnp.bfloat16)
        rs_copy(k, c, 4).start()
        rs_copy(k, c, 1).wait_recv()
        r = rows(part, k, c, right, HR, HR)
        r[...] = (r[...].astype(jnp.float32) + rb[k, c].astype(jnp.float32)).astype(jnp.bfloat16)
        rs_copy(k, c, 5).start()

    def finish(k, c):
        f32 = jnp.float32
        for half, kinds in ((0, (3, 4)), (1, (2, 5))):
            for kind in kinds:
                rs_copy(k, c, kind).wait_recv()
            at = pl.ds(half * HR, HR)
            total = (
                rows(part, k, c, t, half * HR, HR)[...].astype(f32)
                + fl[k, c, at].astype(f32)
                + fr[k, c, at].astype(f32)
            )
            y[k, c, at] = (x[k, c, at].astype(f32) + total).astype(jnp.bfloat16)
            hop(k, c, half, y).start()

    def wait_x1(c):
        @pl.when(s == 0)
        def _():
            inc_load(c).wait()

        @pl.when(s != 0)
        def _():
            for half in range(2):
                hop(0, c, half, y).wait_recv()

    def first(c):
        wait_x1(c)
        norm(1, c)
        ag_start(1, c)

    sums_copy = pltpu.make_async_copy(sum_buf, sums, sum_sem)

    def sum_lists():
        for slot, root in ((0, last), (1, last - 1)):

            @pl.when(s != root)
            def _():
                pool_bcast(slot, 0).wait_recv()

        own = sum_buf.shape[0]
        mine = ((s * NT + t) * own + lax.broadcasted_iota(jnp.int32, (own, HEAD), 0)).astype(jnp.float32)
        total = jnp.zeros((own, dim), jnp.float32)
        for slot in range(2):
            for p in range(3):
                hit = mine == pool[slot, p : p + 1, dim : dim + HEAD]
                hit = jnp.where(hit, 1.0, 0.0)[:, :1]
                total = total + hit * pool[slot, p : p + 1, 0:dim]
        sum_buf[...] = total
        sums_copy.start()

    def wait_tokens():
        @pl.when(s != 0)
        def _():
            tok_copy.wait_recv()

    def gather_phase(k, ahead):
        def step(c, _):
            forward(k, c)

            @pl.when(c + ahead < NC)
            def _():
                if k == 1:
                    wait_x1(c + ahead)
                    norm(k, c + ahead)
                ag_start(k, c + ahead)

            @pl.when(c >= 1)
            def _():
                wait_opp(k, c - 1)
                keys_values(k, c - 1)
                queries(k, c - 1)

            if k == 0:

                @pl.when(c == 1)
                def _():
                    wait_tokens()
                    setup(1)

            return 0

        lax.fori_loop(0, NC, step, 0)
        wait_opp(k, NC - 1)
        keys_values(k, NC - 1)

    def reduce_phase(k):
        def step(c, _):
            attention(k, c)
            project(k, c)

            @pl.when(c == 0)
            def _():
                queries(k, NC - 1)

            @pl.when(c >= 1)
            def _():
                add_on(k, c - 1)

            @pl.when(c >= 2)
            def _():
                finish(k, c - 2)

            return 0

        lax.fori_loop(0, NC, step, 0)
        if k == 0:
            first(0)
        add_on(k, NC - 1)
        finish(k, NC - 2)
        if k == 0:
            first(1)
        finish(k, NC - 1)

    @pl.when(active)
    def _():
        ag_start(0, 0)
        ag_start(0, 1)
        for load in tables:
            load.wait()
        setup(0)
        for load in loads[:3]:
            load.wait()
        gather_phase(0, 2)
        loads[3].wait()
        reduce_phase(0)
        sum_lists()
        gather_phase(1, 2)
        reduce_phase(1)

        def drain(i, _):
            c, k = lax.rem(i, NC), lax.div(i, NC)
            for kind in range(4):
                ag_send(k, c, kind).wait_send()
            for kind in range(6):
                rs_copy(k, c, kind).wait_send()
            return 0

        lax.fori_loop(0, 2 * NC, drain, 0)

    @pl.when(jnp.logical_not(active))
    def _():
        for c in range(NC):

            @pl.when(s != last)
            def _():
                for half in range(2):
                    hop(0, c, half, x).start()

        for slot, root in ((0, last), (1, last - 1)):

            @pl.when(s == root)
            def _():
                pool_root(slot)

        for c in range(NC):
            for half in range(2):
                hop(0, c, half, x).wait_recv()

            @pl.when(s != last)
            def _():
                for half in range(2):
                    hop(1, c, half, x).start()

        wait_tokens()
        sum_lists()

        for slot, root in ((0, last), (1, last - 1)):

            @pl.when(s == root)
            def _():
                def done(j, _):
                    pool_bcast(slot, j).wait_send()
                    return 0

                lax.fori_loop(1, n_sections, done, 0)
                for d in range(1, NT):
                    pool_parts(d).wait_send()

    sums_copy.wait()

    @pl.when(s != last)
    def _():
        tok_copy.wait_send()
        for k in range(2):
            for c in range(NC):
                for half in range(2):
                    hop(k, c, half, y).wait_send()

    @pl.when(s != 0)
    def _():
        for c in range(NC):
            for half in range(2):
                hop(1, c, half, y).wait_recv()

    @pl.when(s == 0)
    def _():
        inc_out.wait()


def solution(mesh):
    n_sections = mesh.shape["section"]
    n_layers = min(n_sections, LAYERS)
    cos_np, sin_np = rope_tables()

    def local(
        flight_state,
        flight_tokens,
        flight_lists,
        incoming,
        incoming_tokens,
        norm_gain,
        query_weight,
        query_bias,
        key_weight,
        key_bias,
        value_weight,
        value_bias,
        output_weight,
        list_rows,
    ):
        dim = flight_state.shape[-1]
        qcols = query_weight.shape[-1]
        heads = qcols // HEAD
        own = list_rows.shape[0] // (n_sections * NT)
        bf16, f32 = jnp.bfloat16, jnp.float32
        dma = pltpu.SemaphoreType.DMA
        hbm = pl.BlockSpec(memory_space=pl.ANY)
        vmem = pl.BlockSpec(memory_space=pltpu.VMEM)
        smem = pl.BlockSpec(memory_space=pltpu.SMEM)

        def body(*refs):
            kernel(n_sections, n_layers, *refs)

        state, sums = pl.pallas_call(
            body,
            out_shape=(
                jax.ShapeDtypeStruct(flight_state.shape, bf16),
                jax.ShapeDtypeStruct((own, dim), f32),
            ),
            in_specs=[
                hbm, smem, smem, hbm, smem, vmem, hbm, vmem, hbm, vmem, hbm, vmem, hbm, smem, hbm, hbm,
            ],
            out_specs=(hbm, hbm),
            scratch_shapes=[
                pltpu.VMEM((dim, qcols + 2 * HEAD), bf16),
                pltpu.VMEM((qcols, dim), bf16),
                pltpu.VMEM((2, NC, CR, dim), bf16),
                pltpu.VMEM((2, NC, CR, dim), bf16),
                pltpu.VMEM((2, NC, NT * CR, dim), bf16),
                pltpu.VMEM((2, NC, NT * CR, dim), bf16),
                pltpu.VMEM((2, NC, HR, dim), bf16),
                pltpu.VMEM((2, NC, HR, dim), bf16),
                pltpu.VMEM((2, NC, CR, dim), bf16),
                pltpu.VMEM((2, NC, CR, dim), bf16),
                pltpu.VMEM((NC, NT, heads * CR, HEAD), bf16),
                pltpu.VMEM((NT * BLOCK, HEAD), bf16),
                pltpu.VMEM((NT * BLOCK, HEAD), bf16),
                pltpu.VMEM((NT * CR, qcols), bf16),
                pltpu.VMEM((2, NC, NT * CR, HEAD), f32),
                pltpu.VMEM((2, NC, NT * CR, HEAD), f32),
                pltpu.VMEM((2, 8, NT * BLOCK), f32),
                pltpu.VMEM((2, 8, HEAD), jnp.int32),
                pltpu.VMEM((2, 8, dim + HEAD), f32),
                pltpu.VMEM((NT, 8, dim), f32),
                dma((4,)),
                dma((NC,)),
                dma((NC + 1,)),
                dma((2, NC, 4)),
                dma((2, NC, 4)),
                dma((2, NC, 6)),
                dma((2, NC, 6)),
                dma((2, NC, 2)),
                dma((2, NC, 2)),
                dma,
                dma,
                dma((NT - 1,)),
                dma((NT - 1,)),
                dma((n_sections,)),
                dma((2,)),
                pltpu.VMEM((own, dim), f32),
                dma,
                pltpu.VMEM((2 * BLOCK, HEAD), f32),
                pltpu.VMEM((2 * BLOCK, HEAD), f32),
                dma((2,)),
            ],
            compiler_params=pltpu.CompilerParams(
                collective_id=0,
                has_side_effects=True,
                vmem_limit_bytes=60 * 1024 * 1024,
            ),
        )(
            flight_state,
            flight_tokens,
            flight_lists,
            incoming,
            incoming_tokens,
            norm_gain,
            query_weight,
            query_bias,
            key_weight,
            key_bias,
            value_weight,
            value_bias,
            output_weight,
            list_rows,
            jnp.asarray(cos_np),
            jnp.asarray(sin_np),
        )

        def write(state_in, sums_in, state_out, sums_out):
            state_out[...] = state_in[...]
            sums_out[...] = sums_in[...]

        steps = 2
        one = pl.BlockSpec((1, BLOCK // steps, dim), lambda i: (0, i, 0))
        two = pl.BlockSpec((own, dim), lambda i: (0, 0))
        return pl.pallas_call(
            write,
            grid=(steps,),
            out_shape=(
                jax.ShapeDtypeStruct(flight_state.shape, bf16),
                jax.ShapeDtypeStruct((own, dim), f32),
            ),
            in_specs=[one, two],
            out_specs=(one, two),
        )(state, sums)

    in_specs = (
        P("section", "tensor", None),
        P("section", None),
        P("section", None),
        P(None, "tensor", None),
        P(),
        P("section", None),
        P("section", None, "tensor"),
        P("section", "tensor"),
        P("section", None, "tensor"),
        P("section", "tensor"),
        P("section", None, "tensor"),
        P("section", "tensor"),
        P("section", "tensor", None),
        P(),
    )
    out_specs = (P("section", "tensor", None), P(("section", "tensor"), None))
    return jax.shard_map(local, mesh=mesh, in_specs=in_specs, out_specs=out_specs, check_vma=False)
```

```python
import math

import jax
import jax.numpy as jnp
import numpy as np
from jax import lax
from jax.experimental import pallas as pl
from jax.experimental.pallas import tpu as pltpu
from jax.sharding import PartitionSpec as P

HEAD = 128
LAYERS = 28
BLOCK = 128
EPS = 1e-06
THETA = 1000000.0

NT = 4
NC = 4
CR = BLOCK // NC
HR = CR // 2
NEG = -1e30
MESH = pl.DeviceIdType.MESH


def rope_tables():
    half = HEAD // 2
    freq = THETA ** (-np.arange(half, dtype=np.float64) * 2.0 / HEAD)
    freq = freq.astype(np.float32).astype(np.float64)
    angle = np.arange(2 * BLOCK, dtype=np.float64)[:, None] * freq[None, :]
    cosine, sine = np.cos(angle), np.sin(angle)
    return (
        np.concatenate([cosine, cosine], 1).astype(np.float32),
        np.concatenate([-sine, sine], 1).astype(np.float32),
    )


def kernel(
    n_sections,
    n_layers,
    flight,
    tokens,
    lists,
    incoming,
    inc_tokens,
    gain,
    wq_hbm,
    qb,
    wk_hbm,
    kb,
    wv_hbm,
    vb,
    wo_hbm,
    list_rows,
    cos_hbm,
    sin_hbm,
    out,
    sums,
    w,
    wo,
    x,
    y,
    g,
    part,
    ra,
    rb,
    fl,
    fr,
    q_s,
    k_s,
    v_s,
    mixed,
    rc,
    rs,
    mask,
    tok,
    pool,
    pool_part,
    w_sem,
    x_sem,
    inc_sem,
    ag_s,
    ag_r,
    rs_s,
    rs_r,
    hop_s,
    hop_r,
    tok_s,
    tok_r,
    pp_s,
    pp_r,
    pb_s,
    pb_r,
    sum_buf,
    sum_sem,
    cos_tab,
    sin_tab,
    tab_sem,
):
    s = lax.axis_index("section")
    t = lax.axis_index("tensor")
    right, left, opp = lax.rem(t + 1, NT), lax.rem(t + 3, NT), lax.rem(t + 2, NT)
    nxt, prv = lax.rem(s + 1, n_sections), lax.rem(s + n_sections - 1, n_sections)
    last = n_sections - 1
    active = s < n_layers
    dim = gain.shape[1]
    qcols = qb.shape[1]
    heads = qcols // HEAD

    def rows(ref, k, c, b, first=0, count=CR):
        return ref.at[k, c, pl.ds(pl.multiple_of(b * CR + first, HR), count)]

    def norm(k, c):
        v = x[k, c].astype(jnp.float32)
        scale = lax.rsqrt(jnp.mean(v * v, axis=-1, keepdims=True) + EPS)
        rows(g, k, c, t)[...] = (v * scale * gain[...]).astype(jnp.bfloat16)

    loads = [
        pltpu.make_async_copy(wk_hbm.at[0], w.at[:, pl.ds(0, HEAD)], w_sem.at[0]),
        pltpu.make_async_copy(wv_hbm.at[0], w.at[:, pl.ds(HEAD, HEAD)], w_sem.at[1]),
        pltpu.make_async_copy(wq_hbm.at[0], w.at[:, pl.ds(2 * HEAD, qcols)], w_sem.at[2]),
        pltpu.make_async_copy(wo_hbm.at[0], wo, w_sem.at[3]),
    ]

    tables = [
        pltpu.make_async_copy(cos_hbm, cos_tab, tab_sem.at[0]),
        pltpu.make_async_copy(sin_hbm, sin_tab, tab_sem.at[1]),
    ]

    def x_load(c):
        return pltpu.make_async_copy(
            flight.at[0, pl.ds(c * CR, CR)], x.at[0, c], x_sem.at[c]
        )

    def inc_load(c):
        return pltpu.make_async_copy(
            incoming.at[0, pl.ds(c * CR, CR)], x.at[1, c], inc_sem.at[c]
        )

    inc_out = pltpu.make_async_copy(incoming.at[1], out.at[0], inc_sem.at[NC])

    for c in range(NC):
        x_load(c).start()

    @pl.when(active)
    def _():
        for load in tables + loads:
            load.start()

    @pl.when(s == 0)
    def _():
        for c in range(NC):
            inc_load(c).start()
        inc_out.start()

    bar = pltpu.get_barrier_semaphore()
    for peer in (left, right, opp):
        pl.semaphore_signal(bar, inc=1, device_id=(s, peer), device_id_type=MESH)
    pl.semaphore_signal(bar, inc=1, device_id=(prv, t), device_id_type=MESH)
    for root in (last - 1, last):

        @pl.when(s != root)
        def _():
            pl.semaphore_signal(bar, inc=1, device_id=(root, t), device_id_type=MESH)

    for c in range(NC):
        x_load(c).wait()

    @pl.when(active)
    def _():
        for c in range(NC):
            norm(0, c)

    @pl.when(s < last - 1)
    def _():
        pl.semaphore_wait(bar, 4)

    @pl.when(s >= last - 1)
    def _():
        pl.semaphore_wait(bar, 4 + n_sections - 1)

    row8 = lax.broadcasted_iota(jnp.int32, (8, HEAD), 0)

    def token_rows(ref):
        return jnp.where(
            row8 == 0, ref[0, 0], jnp.where(row8 == 1, ref[0, 1], ref[0, 2])
        )

    tok[0] = token_rows(tokens)
    tok_copy = pltpu.make_async_remote_copy(
        tok.at[0], tok.at[1], tok_s, tok_r, device_id=(nxt, t), device_id_type=MESH
    )

    @pl.when(s != last)
    def _():
        tok_copy.start()

    @pl.when(s == 0)
    def _():
        tok[1] = token_rows(inc_tokens)

    def layout(k, b):
        n = [tok[k, p : p + 1, :] for p in range(3)]
        e0 = jnp.where(n[0] > BLOCK, 2, 1)
        e1 = e0 + jnp.where(n[1] > BLOCK, 2, 1)
        prog = jnp.where(b >= e0, 1, 0) + jnp.where(b >= e1, 1, 0)
        begin = jnp.where(prog == 0, 0, jnp.where(prog == 1, e0, e1))
        length = jnp.where(prog == 0, n[0], jnp.where(prog == 1, n[1], n[2]))
        return prog, b - begin, length

    def remote(src, dst, ssem, rsem, dev):
        return pltpu.make_async_remote_copy(
            src, dst, ssem, rsem, device_id=dev, device_id_type=MESH
        )

    def ag_send(k, c, kind):
        if kind == 0:
            r, dev = rows(g, k, c, t), (s, right)
        elif kind == 1:
            r, dev = rows(g, k, c, t), (s, left)
        elif kind == 2:
            r, dev = rows(g, k, c, left, 0, HR), (s, right)
        else:
            r, dev = rows(g, k, c, right, HR, HR), (s, left)
        return remote(r, r, ag_s.at[k, c, kind], ag_r.at[k, c, kind], dev)

    def ag_recv(k, c, kind):
        if kind == 0:
            r, dev = rows(g, k, c, left), (s, left)
        elif kind == 1:
            r, dev = rows(g, k, c, right), (s, right)
        elif kind == 2:
            r, dev = rows(g, k, c, opp, 0, HR), (s, left)
        else:
            r, dev = rows(g, k, c, opp, HR, HR), (s, right)
        return remote(r, r, ag_s.at[k, c, kind], ag_r.at[k, c, kind], dev)

    def rs_copy(k, c, kind):
        if kind == 0:
            src, dst, dev = rows(part, k, c, opp, 0, HR), ra.at[k, c], (s, left)
        elif kind == 1:
            src, dst, dev = rows(part, k, c, opp, HR, HR), rb.at[k, c], (s, right)
        elif kind == 2:
            src, dst, dev = rows(part, k, c, left, HR, HR), fr.at[k, c, pl.ds(HR, HR)], (s, left)
        elif kind == 3:
            src, dst, dev = rows(part, k, c, right, 0, HR), fl.at[k, c, pl.ds(0, HR)], (s, right)
        elif kind == 4:
            src, dst, dev = rows(part, k, c, left, 0, HR), fr.at[k, c, pl.ds(0, HR)], (s, left)
        else:
            src, dst, dev = rows(part, k, c, right, HR, HR), fl.at[k, c, pl.ds(HR, HR)], (s, right)
        return remote(src, dst, rs_s.at[k, c, kind], rs_r.at[k, c, kind], dev)

    def hop(k, c, half, src):
        if k == 0:
            dst = x.at[1, c, pl.ds(half * HR, HR)]
        else:
            dst = out.at[0, pl.ds(pl.multiple_of(c * CR + half * HR, HR), HR)]
        src = src.at[k, c, pl.ds(half * HR, HR)]
        return remote(src, dst, hop_s.at[k, c, half], hop_r.at[k, c, half], (nxt, t))

    lane_row = lax.broadcasted_iota(jnp.int32, (8, HEAD), 1)

    def pool_bcast(slot, j):
        dev = (lax.rem(s + j, n_sections), t)
        return remote(pool.at[slot], pool.at[slot], pb_s.at[j], pb_r.at[slot], dev)

    def pool_parts(d):
        dev = (s, lax.rem(t + d, NT))
        return remote(pool_part.at[0], pool_part.at[d], pp_s.at[d - 1], pp_r.at[d - 1], dev)

    def pool_root(slot):
        prog, second, length = layout(0, t)
        member = (row8 == prog) & (lane_row + BLOCK * second < length)
        member = jnp.where(member, 1.0, 0.0).astype(jnp.bfloat16)
        whole = x[0].reshape(BLOCK, dim)
        pool_part[0] = jnp.dot(member, whole, preferred_element_type=jnp.float32)
        for d in range(1, NT):
            pool_parts(d).start()
        for d in range(1, NT):
            pool_parts(d).wait_recv()
        total = pool_part[0] + pool_part[1] + pool_part[2] + pool_part[3]
        count = tok[0][:, :1].astype(jnp.float32)
        mean = total / count
        emb = mean * lax.rsqrt(jnp.mean(mean * mean, axis=-1, keepdims=True) + EPS)
        pool[slot, :, 0:dim] = emb
        target = [list_rows[lists[0, p]] for p in range(3)]
        target = jnp.where(
            row8 == 0, target[0], jnp.where(row8 == 1, target[1], target[2])
        )
        target = jnp.where(row8 < 3, target, -1)
        pool[slot, :, dim : dim + HEAD] = target.astype(jnp.float32)

        def send(j, _):
            pool_bcast(slot, j).start()
            return 0

        lax.fori_loop(1, n_sections, send, 0)

    def setup(k):
        i = lax.broadcasted_iota(jnp.int32, (1, HEAD), 1)
        info = [layout(k, b) for b in range(NT)]
        for b in range(NT):
            for kb_ in range(NT):
                ok = (info[b][0] == info[kb_][0]) & (i + BLOCK * info[kb_][1] < info[kb_][2])
                mask[k, b : b + 1, kb_ * BLOCK : (kb_ + 1) * BLOCK] = jnp.where(ok, 0.0, NEG)
        for b in range(NT):
            second = info[b][1] > 0
            for c in range(NC):
                lo, hi = c * CR, (c + 1) * CR
                rc[k, c, b * CR : (b + 1) * CR] = jnp.where(
                    second, cos_tab[BLOCK + lo : BLOCK + hi], cos_tab[lo:hi]
                )
                rs[k, c, b * CR : (b + 1) * CR] = jnp.where(
                    second, sin_tab[BLOCK + lo : BLOCK + hi], sin_tab[lo:hi]
                )

    def ag_start(k, c):
        ag_send(k, c, 0).start()
        ag_send(k, c, 1).start()

    def forward(k, c):
        ag_recv(k, c, 0).wait_recv()
        ag_send(k, c, 2).start()
        ag_recv(k, c, 1).wait_recv()
        ag_send(k, c, 3).start()

    def wait_opp(k, c):
        ag_recv(k, c, 2).wait_recv()
        ag_recv(k, c, 3).wait_recv()

    def rope(v, k, c):
        return (v * rc[k, c] + pltpu.roll(v, HEAD // 2, 1) * rs[k, c]).astype(jnp.bfloat16)

    def keys_values(k, c):
        kv = jnp.dot(g[k, c], w[:, 0 : 2 * HEAD], preferred_element_type=jnp.float32)
        key = rope(kv[:, :HEAD] + kb[...], k, c)
        val = (kv[:, HEAD:] + vb[...]).astype(jnp.bfloat16)
        for b in range(NT):
            at = pl.ds(pl.multiple_of(b * BLOCK + c * CR, CR), CR)
            k_s[at, :] = key[b * CR : (b + 1) * CR]
            v_s[at, :] = val[b * CR : (b + 1) * CR]

    def queries(k, c):
        lhs = g[k, c]
        for h0 in range(0, heads, 2):
            n = min(2, heads - h0)
            q = jnp.dot(
                lhs,
                w[:, (2 + h0) * HEAD : (2 + h0 + n) * HEAD],
                preferred_element_type=jnp.float32,
            )
            for j in range(n):
                h = h0 + j
                v = q[:, j * HEAD : (j + 1) * HEAD] + qb[:, h * HEAD : (h + 1) * HEAD]
                v = rope(v, k, c)
                for b in range(NT):
                    q_s[c, b, h * CR : (h + 1) * CR, :] = v[b * CR : (b + 1) * CR]

    def attention(k, c):
        scale = 1.0 / math.sqrt(HEAD)
        spans = [(max(b - 1, 0) * BLOCK, min(b + 2, NT) * BLOCK) for b in range(NT)]
        scores = [
            lax.dot_general(
                q_s[c, b],
                k_s[lo:hi, :],
                (((1,), (1,)), ((), ())),
                preferred_element_type=jnp.float32,
            )
            for b, (lo, hi) in enumerate(spans)
        ]
        outs = []
        for b, (lo, hi) in enumerate(spans):
            sc = scores[b] * scale + mask[k, b : b + 1, lo:hi]
            e = jnp.exp(sc - jnp.max(sc, axis=-1, keepdims=True))
            p = (e * (1.0 / jnp.sum(e, axis=-1, keepdims=True))).astype(jnp.bfloat16)
            o = jnp.dot(p, v_s[lo:hi, :], preferred_element_type=jnp.float32)
            outs.append(o.astype(jnp.bfloat16))
        for b in range(NT):
            for h in range(heads):
                mixed[b * CR : (b + 1) * CR, h * HEAD : (h + 1) * HEAD] = outs[b][
                    h * CR : (h + 1) * CR
                ]

    def project(k, c):
        width = 512
        lhs = mixed[...]
        for n in range(0, dim, width):
            part[k, c, :, n : n + width] = jnp.dot(
                lhs, wo[:, n : n + width], preferred_element_type=jnp.float32
            ).astype(jnp.bfloat16)
        for kind in range(4):
            rs_copy(k, c, kind).start()

    def add_on(k, c):
        rs_copy(k, c, 0).wait_recv()
        r = rows(part, k, c, left, 0, HR)
        r[...] = (r[...].astype(jnp.float32) + ra[k, c].astype(jnp.float32)).astype(jnp.bfloat16)
        rs_copy(k, c, 4).start()
        rs_copy(k, c, 1).wait_recv()
        r = rows(part, k, c, right, HR, HR)
        r[...] = (r[...].astype(jnp.float32) + rb[k, c].astype(jnp.float32)).astype(jnp.bfloat16)
        rs_copy(k, c, 5).start()

    def finish(k, c):
        f32 = jnp.float32
        for half, kinds in ((0, (3, 4)), (1, (2, 5))):
            for kind in kinds:
                rs_copy(k, c, kind).wait_recv()
            at = pl.ds(half * HR, HR)
            total = (
                rows(part, k, c, t, half * HR, HR)[...].astype(f32)
                + fl[k, c, at].astype(f32)
                + fr[k, c, at].astype(f32)
            )
            y[k, c, at] = (x[k, c, at].astype(f32) + total).astype(jnp.bfloat16)
            hop(k, c, half, y).start()

    def wait_x1(c):
        @pl.when(s == 0)
        def _():
            inc_load(c).wait()

        @pl.when(s != 0)
        def _():
            for half in range(2):
                hop(0, c, half, y).wait_recv()

    def first(c):
        wait_x1(c)
        norm(1, c)
        ag_start(1, c)

    sums_copy = pltpu.make_async_copy(sum_buf, sums, sum_sem)

    def sum_lists():
        for slot, root in ((0, last), (1, last - 1)):

            @pl.when(s != root)
            def _():
                pool_bcast(slot, 0).wait_recv()

        own = sum_buf.shape[0]
        mine = ((s * NT + t) * own + lax.broadcasted_iota(jnp.int32, (own, HEAD), 0)).astype(jnp.float32)
        total = jnp.zeros((own, dim), jnp.float32)
        for slot in range(2):
            for p in range(3):
                hit = mine == pool[slot, p : p + 1, dim : dim + HEAD]
                hit = jnp.where(hit, 1.0, 0.0)[:, :1]
                total = total + hit * pool[slot, p : p + 1, 0:dim]
        sum_buf[...] = total
        sums_copy.start()

    def wait_tokens():
        @pl.when(s != 0)
        def _():
            tok_copy.wait_recv()

    def gather_phase(k, ahead):
        def step(c, _):
            forward(k, c)

            @pl.when(c + ahead < NC)
            def _():
                if k == 1:
                    wait_x1(c + ahead)
                    norm(k, c + ahead)
                ag_start(k, c + ahead)

            @pl.when(c >= 1)
            def _():
                wait_opp(k, c - 1)
                keys_values(k, c - 1)
                queries(k, c - 1)

            if k == 0:

                @pl.when(c == 1)
                def _():
                    wait_tokens()
                    setup(1)

            return 0

        lax.fori_loop(0, NC, step, 0)
        wait_opp(k, NC - 1)
        keys_values(k, NC - 1)

    def reduce_phase(k):
        def step(c, _):
            attention(k, c)
            project(k, c)

            @pl.when(c == 0)
            def _():
                queries(k, NC - 1)

            @pl.when(c >= 1)
            def _():
                add_on(k, c - 1)

            if k == 0:

                @pl.when(c == NC - 1)
                def _():
                    first(0)

            @pl.when(c >= 2)
            def _():
                finish(k, c - 2)

            return 0

        lax.fori_loop(0, NC, step, 0)
        add_on(k, NC - 1)
        finish(k, NC - 2)
        if k == 0:
            first(1)
        finish(k, NC - 1)

    @pl.when(active)
    def _():
        ag_start(0, 0)
        ag_start(0, 1)
        for load in tables:
            load.wait()
        setup(0)
        for load in loads[:3]:
            load.wait()
        gather_phase(0, 2)
        loads[3].wait()
        reduce_phase(0)
        sum_lists()
        gather_phase(1, 2)
        reduce_phase(1)

        def drain(i, _):
            c, k = lax.rem(i, NC), lax.div(i, NC)
            for kind in range(4):
                ag_send(k, c, kind).wait_send()
            for kind in range(6):
                rs_copy(k, c, kind).wait_send()
            return 0

        lax.fori_loop(0, 2 * NC, drain, 0)

    @pl.when(jnp.logical_not(active))
    def _():
        for c in range(NC):

            @pl.when(s != last)
            def _():
                for half in range(2):
                    hop(0, c, half, x).start()

        for slot, root in ((0, last), (1, last - 1)):

            @pl.when(s == root)
            def _():
                pool_root(slot)

        for c in range(NC):
            for half in range(2):
                hop(0, c, half, x).wait_recv()

            @pl.when(s != last)
            def _():
                for half in range(2):
                    hop(1, c, half, x).start()

        wait_tokens()
        sum_lists()

        for slot, root in ((0, last), (1, last - 1)):

            @pl.when(s == root)
            def _():
                def done(j, _):
                    pool_bcast(slot, j).wait_send()
                    return 0

                lax.fori_loop(1, n_sections, done, 0)
                for d in range(1, NT):
                    pool_parts(d).wait_send()

    sums_copy.wait()

    @pl.when(s != last)
    def _():
        tok_copy.wait_send()
        for k in range(2):
            for c in range(NC):
                for half in range(2):
                    hop(k, c, half, y).wait_send()

    @pl.when(s != 0)
    def _():
        for c in range(NC):
            for half in range(2):
                hop(1, c, half, y).wait_recv()

    @pl.when(s == 0)
    def _():
        inc_out.wait()


def solution(mesh):
    n_sections = mesh.shape["section"]
    n_layers = min(n_sections, LAYERS)
    cos_np, sin_np = rope_tables()

    def local(
        flight_state,
        flight_tokens,
        flight_lists,
        incoming,
        incoming_tokens,
        norm_gain,
        query_weight,
        query_bias,
        key_weight,
        key_bias,
        value_weight,
        value_bias,
        output_weight,
        list_rows,
    ):
        dim = flight_state.shape[-1]
        qcols = query_weight.shape[-1]
        heads = qcols // HEAD
        own = list_rows.shape[0] // (n_sections * NT)
        bf16, f32 = jnp.bfloat16, jnp.float32
        dma = pltpu.SemaphoreType.DMA
        hbm = pl.BlockSpec(memory_space=pl.ANY)
        vmem = pl.BlockSpec(memory_space=pltpu.VMEM)
        smem = pl.BlockSpec(memory_space=pltpu.SMEM)

        def body(*refs):
            kernel(n_sections, n_layers, *refs)

        state, sums = pl.pallas_call(
            body,
            out_shape=(
                jax.ShapeDtypeStruct(flight_state.shape, bf16),
                jax.ShapeDtypeStruct((own, dim), f32),
            ),
            in_specs=[
                hbm, smem, smem, hbm, smem, vmem, hbm, vmem, hbm, vmem, hbm, vmem, hbm, smem, hbm, hbm,
            ],
            out_specs=(hbm, hbm),
            scratch_shapes=[
                pltpu.VMEM((dim, qcols + 2 * HEAD), bf16),
                pltpu.VMEM((qcols, dim), bf16),
                pltpu.VMEM((2, NC, CR, dim), bf16),
                pltpu.VMEM((2, NC, CR, dim), bf16),
                pltpu.VMEM((2, NC, NT * CR, dim), bf16),
                pltpu.VMEM((2, NC, NT * CR, dim), bf16),
                pltpu.VMEM((2, NC, HR, dim), bf16),
                pltpu.VMEM((2, NC, HR, dim), bf16),
                pltpu.VMEM((2, NC, CR, dim), bf16),
                pltpu.VMEM((2, NC, CR, dim), bf16),
                pltpu.VMEM((NC, NT, heads * CR, HEAD), bf16),
                pltpu.VMEM((NT * BLOCK, HEAD), bf16),
                pltpu.VMEM((NT * BLOCK, HEAD), bf16),
                pltpu.VMEM((NT * CR, qcols), bf16),
                pltpu.VMEM((2, NC, NT * CR, HEAD), f32),
                pltpu.VMEM((2, NC, NT * CR, HEAD), f32),
                pltpu.VMEM((2, 8, NT * BLOCK), f32),
                pltpu.VMEM((2, 8, HEAD), jnp.int32),
                pltpu.VMEM((2, 8, dim + HEAD), f32),
                pltpu.VMEM((NT, 8, dim), f32),
                dma((4,)),
                dma((NC,)),
                dma((NC + 1,)),
                dma((2, NC, 4)),
                dma((2, NC, 4)),
                dma((2, NC, 6)),
                dma((2, NC, 6)),
                dma((2, NC, 2)),
                dma((2, NC, 2)),
                dma,
                dma,
                dma((NT - 1,)),
                dma((NT - 1,)),
                dma((n_sections,)),
                dma((2,)),
                pltpu.VMEM((own, dim), f32),
                dma,
                pltpu.VMEM((2 * BLOCK, HEAD), f32),
                pltpu.VMEM((2 * BLOCK, HEAD), f32),
                dma((2,)),
            ],
            compiler_params=pltpu.CompilerParams(
                collective_id=0,
                has_side_effects=True,
                vmem_limit_bytes=60 * 1024 * 1024,
            ),
        )(
            flight_state,
            flight_tokens,
            flight_lists,
            incoming,
            incoming_tokens,
            norm_gain,
            query_weight,
            query_bias,
            key_weight,
            key_bias,
            value_weight,
            value_bias,
            output_weight,
            list_rows,
            jnp.asarray(cos_np),
            jnp.asarray(sin_np),
        )

        def write(state_in, sums_in, state_out, sums_out):
            state_out[...] = state_in[...]
            sums_out[...] = sums_in[...]

        steps = 2
        one = pl.BlockSpec((1, BLOCK // steps, dim), lambda i: (0, i, 0))
        two = pl.BlockSpec((own, dim), lambda i: (0, 0))
        return pl.pallas_call(
            write,
            grid=(steps,),
            out_shape=(
                jax.ShapeDtypeStruct(flight_state.shape, bf16),
                jax.ShapeDtypeStruct((own, dim), f32),
            ),
            in_specs=[one, two],
            out_specs=(one, two),
        )(state, sums)

    in_specs = (
        P("section", "tensor", None),
        P("section", None),
        P("section", None),
        P(None, "tensor", None),
        P(),
        P("section", None),
        P("section", None, "tensor"),
        P("section", "tensor"),
        P("section", None, "tensor"),
        P("section", "tensor"),
        P("section", None, "tensor"),
        P("section", "tensor"),
        P("section", "tensor", None),
        P(),
    )
    out_specs = (P("section", "tensor", None), P(("section", "tensor"), None))
    return jax.shard_map(local, mesh=mesh, in_specs=in_specs, out_specs=out_specs, check_vma=False)
```
